256 devices in a mesh: frame: 8 (over y, core), row: 32 (over z, x).
Axes of the slice: x: 4, y: 4, z: 8, core: 2. Of those that a mesh axis runs over, the one named last changes fastest.
Arguments:
- latents: bfloat16 [16, 32, 106, 320], P('frame', 'row'), may hold values from -6 to 6
- segments: int32 [16], replicated, may hold values from 0 to 7, never falling along the last dimension, each value on 1 to 6 neighbouring positions
- w_spatial: bfloat16 [3, 3, 320, 320], replicated, may hold values from -0.109375 to 0.109375
- w_temporal: bfloat16 [3, 320, 320], replicated, may hold values from -0.1875 to 0.1875
- w_qkv: bfloat16 [320, 960], replicated, may hold values from -3 to 3, as said below
- w_out: bfloat16 [320, 320], replicated, may hold values from -0.3125 to 0.3125
- cotangent: bfloat16 [16, 32, 106, 320], P('frame', 'row'), may hold values from -6 to 6
Outputs:
- grad_input: bfloat16 [16, 32, 106, 320], P('frame', 'row')
- grad_w_spatial: float32 [3, 3, 320, 320], replicated
- grad_w_temporal: float32 [3, 320, 320], replicated
- grad_w_qkv: float32 [320, 960], replicated
- grad_w_out: float32 [320, 320], replicated
The draws below stay inside these ranges and needn't reach their ends.
Inputs may be any that keep to these rules, and one draw needn't show every extreme that they name: `w_qkv`: projection weights between -3 and 3.
All inputs are finite; a program needn't handle non-finite values.
Results may differ from the reference program's by a relative error of at most 0.02.
Values may be sent and summed in bfloat16 or wider, within the bound.
A program may use at most 64 MiB of HBM per device.

```python
import math
import jax
import jax.numpy as jnp
import numpy as np
from jax import lax

C = 320
HEADS = 8
W = 106
FRAMES = 16
H = 32
SHOTS = 8
SHOT_MOST = 6


def draw_w_qkv(key, part):
    key = jax.random.fold_in(key, 11)
    base_key, value_key, other_key = jax.random.split(key, 3)
    spread = C ** (-0.5)
    base = jax.random.normal(base_key, (C, C), jnp.float32) * spread
    values = jax.random.normal(value_key, (C, C), jnp.float32) * spread
    queries = base
    key_cols = jax.random.normal(other_key, (C, C), jnp.float32) * spread
    joined = jnp.concatenate([queries, key_cols, values], axis=1)
    return jnp.clip(joined, -3.0, 3.0).astype(jnp.bfloat16)


def level_of(own_key, extent, cuts, least, largest):
    factor_of = 1.0
    for position, blocks in cuts:
        steps = jax.random.uniform(jax.random.fold_in(jax.random.fold_in(own_key, 6), position), (blocks,), jnp.float32, least / len(cuts), largest / len(cuts))
        factor_of = factor_of * jnp.repeat(jnp.exp(steps), extent[position] // blocks).reshape((-1,) + (1,) * (len(extent) - 1 - position))
    return factor_of


def split_up(amount, total, limit, lean):
    loads = [(1 << 20) // math.isqrt(rank ** lean) + 1 for rank in range(2, amount + 1)]
    rest, counts = total - limit - (amount - 1), [1] * (amount - 1)
    while rest > 0:
        free = [i for i in range(amount - 1) if counts[i] < limit]
        pool, remaining = sum([loads[i] for i in free]), rest
        for i in free:
            addition = min(limit - counts[i], max(1, remaining * loads[i] // pool), rest)
            counts[i] = counts[i] + addition
            rest = rest - addition
    return np.array([limit] + counts)


def ragged(own_key, number_of, total, bound, skew):
    if number_of == 2:
        one = jax.random.randint(own_key, (), max(1, total - bound), min(bound, total - 1) + 1)
        return jnp.stack([one, total - one])
    tallies = jnp.asarray(split_up(number_of, total, bound, skew), jnp.int32)
    twos = (number_of - 1) // 2
    donor, taker = tallies[1:1 + 2 * twos:2], tallies[2:2 + 2 * twos:2]
    room = jnp.minimum(donor - 1, bound - taker)
    moved = jax.random.randint(jax.random.fold_in(own_key, 1), (twos,), 0, 1 << 20) % (room + 1)
    tallies = tallies.at[1:1 + 2 * twos:2].set(donor - moved).at[2:2 + 2 * twos:2].set(taker + moved)
    return tallies[jax.random.permutation(jax.random.fold_in(own_key, 2), number_of)]


def scatter_about(own_key, dims, scale, limit, cuts=(), dtype=jnp.bfloat16):
    loudness = level_of(own_key, dims, cuts, -0.22, 0.18) if cuts else 1.0
    drawn = jax.random.normal(own_key, dims, jnp.float32) * scale * loudness
    return jnp.minimum(jnp.maximum(drawn, -limit), limit).astype(dtype)


def setup_inputs(seed: int = 0) -> dict:
    seeds = jax.random.split(jax.random.key(seed), 8)
    latents = scatter_about(seeds[0], (FRAMES, H, W, C), 1.0, 6.0, ((0, 8), (1, 32)))
    segments = jnp.searchsorted(jnp.cumsum(ragged(seeds[1], SHOTS, FRAMES, SHOT_MOST, 0)), jnp.arange(FRAMES), side="right").astype(jnp.int32)
    w_spatial = scatter_about(seeds[2], (3, 3, C, C), (9 * C) ** -0.5, 0.109375)
    w_temporal = scatter_about(seeds[3], (3, C, C), (3 * C) ** -0.5, 0.1875)
    w_qkv = draw_w_qkv(jax.random.fold_in(seeds[7], 71), 0)
    w_out = scatter_about(seeds[5], (C, C), C ** -0.5, 0.3125)
    cotangent = scatter_about(seeds[6], (FRAMES, H, W, C), 1.0, 6.0, ((0, 8), (1, 32)))
    return dict(latents=latents, segments=segments, w_spatial=w_spatial, w_temporal=w_temporal, w_qkv=w_qkv, w_out=w_out, cotangent=cotangent)


def silu_grad(values):
    sig = jax.nn.sigmoid(values)
    return sig * (1.0 + values * (1.0 - sig))

def project(inputs, weights):
    flat = inputs.reshape(-1, inputs.shape[-1])
    result = jnp.dot(flat, weights, preferred_element_type=jnp.float32)
    return result.reshape(inputs.shape[:-1] + (weights.shape[-1],))

def conv_taps(padded, weights, row_count, col_count):
    summed = jnp.zeros(padded.shape[:1] + (row_count, col_count, weights.shape[-1]), jnp.float32)
    for tap_row in range(3):
        for tap_col in range(3):
            window = padded[:, tap_row:tap_row + row_count, tap_col:tap_col + col_count, :]
            summed = summed + project(window, weights[tap_row, tap_col])
    return summed

def conv_back(d_padded, weights, row_count, col_count):
    summed = jnp.zeros(d_padded.shape[:1] + (row_count, col_count, weights.shape[-2]), jnp.float32)
    for tap_row in range(3):
        for tap_col in range(3):
            window = d_padded[:, 2 - tap_row:2 - tap_row + row_count, 2 - tap_col:2 - tap_col + col_count, :]
            summed = summed + project(window, weights[tap_row, tap_col].T)
    return summed

def spatial_grad(padded, d_out, row_count, col_count):
    channels = padded.shape[-1]
    flat_d = d_out.reshape(-1, d_out.shape[-1])
    taps = []
    for tap_row in range(3):
        for tap_col in range(3):
            window = padded[:, tap_row:tap_row + row_count, tap_col:tap_col + col_count, :].reshape(-1, channels)
            taps.append(jnp.dot(window.T, flat_d, preferred_element_type=jnp.float32))
    return jnp.stack(taps).reshape(3, 3, channels, flat_d.shape[-1])

def pair_product(form, left, right):
    return jnp.einsum(form, left.astype(jnp.float32), right.astype(jnp.float32), precision=lax.Precision.HIGHEST)

def temporal_block(spatial, cotangent, segments, w_temporal, w_qkv, w_out):
    frames, pixels, channels = spatial.shape
    head_count = HEADS
    head_dim = channels // head_count
    score_scale = 1.0 / head_dim ** 0.5
    same_shot = segments[:, None] == segments[None, :]
    next_ok = jnp.concatenate([(segments[1:] == segments[:-1]).astype(jnp.float32), jnp.zeros((1,), jnp.float32)])
    prev_ok = jnp.concatenate([jnp.zeros((1,), jnp.float32), next_ok[:-1]])
    spatial_f = spatial.astype(jnp.float32)
    act_mid = jax.nn.silu(spatial_f).astype(jnp.bfloat16)
    zero_frame = jnp.zeros((1, pixels, channels), jnp.bfloat16)
    prev_t = jnp.concatenate([zero_frame, act_mid[:-1]]) * prev_ok.astype(jnp.bfloat16)[:, None, None]
    next_t = jnp.concatenate([act_mid[1:], zero_frame]) * next_ok.astype(jnp.bfloat16)[:, None, None]
    temporal = (spatial_f + project(prev_t, w_temporal[0]) + project(act_mid, w_temporal[1]) + project(next_t, w_temporal[2])).astype(jnp.bfloat16)
    temporal_f = temporal.astype(jnp.float32)
    centred = temporal_f - lax.optimization_barrier(jnp.mean(temporal_f, axis=-1, keepdims=True))
    inv_std = lax.rsqrt(lax.optimization_barrier(jnp.mean(centred * centred, axis=-1, keepdims=True)) + 1e-05)
    nhat = centred * inv_std
    normed = nhat.astype(jnp.bfloat16)
    qkv_all = project(normed, w_qkv)
    split_shape = (frames, pixels, head_count, head_dim)
    queries = qkv_all[..., :channels].astype(jnp.bfloat16).reshape(split_shape)
    key_vecs = qkv_all[..., channels:2 * channels].astype(jnp.bfloat16).reshape(split_shape)
    values = qkv_all[..., 2 * channels:].astype(jnp.bfloat16).reshape(split_shape)
    scores = pair_product('fphd,gphd->phfg', queries, key_vecs) * score_scale
    scores = jnp.where(same_shot[None, None], scores, -1e+30)
    row_peak = lax.optimization_barrier(jnp.max(scores, axis=-1, keepdims=True))
    expo = jnp.exp(scores - row_peak)
    attn_prob = expo / lax.optimization_barrier(jnp.sum(expo, axis=-1, keepdims=True))
    prob_b = attn_prob.astype(jnp.bfloat16)
    mixed = pair_product('phfg,gphd->fphd', prob_b, values).astype(jnp.bfloat16).reshape(frames, pixels, channels)
    flat_cot = cotangent.reshape(-1, channels)
    grad_out = jnp.dot(mixed.reshape(-1, channels).T, flat_cot, preferred_element_type=jnp.float32)
    d_mixed = project(cotangent, w_out.T).astype(jnp.bfloat16).reshape(split_shape)
    d_prob = pair_product('fphd,gphd->phfg', d_mixed, values)
    d_value = pair_product('phfg,fphd->gphd', prob_b, d_mixed).astype(jnp.bfloat16)
    d_score = (attn_prob * (d_prob - lax.optimization_barrier(jnp.sum(attn_prob * d_prob, axis=-1, keepdims=True))) * score_scale).astype(jnp.bfloat16)
    d_query = pair_product('phfg,gphd->fphd', d_score, key_vecs).astype(jnp.bfloat16)
    d_key = pair_product('phfg,fphd->gphd', d_score, queries).astype(jnp.bfloat16)
    d_qkv = jnp.concatenate([d_query.reshape(frames, pixels, channels), d_key.reshape(frames, pixels, channels), d_value.reshape(frames, pixels, channels)], axis=-1)
    grad_qkv = jnp.dot(normed.reshape(-1, channels).T, d_qkv.reshape(-1, 3 * channels), preferred_element_type=jnp.float32)
    d_normed = project(d_qkv, w_qkv.T)
    ln_back = inv_std * (d_normed - lax.optimization_barrier(jnp.mean(d_normed, axis=-1, keepdims=True)) - nhat * lax.optimization_barrier(jnp.mean(d_normed * nhat, axis=-1, keepdims=True)))
    d_temporal = (cotangent.astype(jnp.float32) + ln_back).astype(jnp.bfloat16)
    flat_dt = d_temporal.reshape(-1, channels)
    grad_time = jnp.stack([jnp.dot(prev_t.reshape(-1, channels).T, flat_dt, preferred_element_type=jnp.float32), jnp.dot(act_mid.reshape(-1, channels).T, flat_dt, preferred_element_type=jnp.float32), jnp.dot(next_t.reshape(-1, channels).T, flat_dt, preferred_element_type=jnp.float32)])
    back_prev = project(d_temporal, w_temporal[0].T)
    back_mid = project(d_temporal, w_temporal[1].T)
    back_next = project(d_temporal, w_temporal[2].T)
    zero_f = jnp.zeros((1, pixels, channels), jnp.float32)
    carried = back_mid + jnp.concatenate([back_prev[1:], zero_f]) * next_ok[:, None, None] + jnp.concatenate([zero_f, back_next[:-1]]) * prev_ok[:, None, None]
    d_spatial = (d_temporal.astype(jnp.float32) + silu_grad(spatial_f) * carried).astype(jnp.bfloat16)
    return (d_spatial, (grad_time, grad_qkv, grad_out))

def reference(latents, segments, w_spatial, w_temporal, w_qkv, w_out, cotangent):
    row_count = latents.shape[1]
    col_count = latents.shape[2]
    channels = latents.shape[3]
    edge = ((0, 0), (1, 1), (1, 1), (0, 0))

    def forward_frame(carry, frame):
        act_in = jax.nn.silu(frame.astype(jnp.float32)).astype(jnp.bfloat16)
        padded = jnp.pad(act_in[None], edge)
        result = (frame.astype(jnp.float32) + conv_taps(padded, w_spatial, row_count, col_count)[0]).astype(jnp.bfloat16)
        return (carry, result)
    _, spatial = lax.scan(forward_frame, jnp.zeros((), jnp.float32), latents)
    spatial_rows = jnp.swapaxes(spatial, 0, 1)
    cot_rows = jnp.swapaxes(cotangent, 0, 1)
    start = (jnp.zeros((3, channels, channels), jnp.float32), jnp.zeros((channels, 3 * channels), jnp.float32), jnp.zeros((channels, channels), jnp.float32))

    def row_step(carry, inputs):
        d_rows, grads = temporal_block(inputs[0], inputs[1], segments, w_temporal, w_qkv, w_out)
        return (jax.tree.map(lambda left, right: left + right, carry, grads), d_rows)
    grads_time, d_rows = lax.scan(row_step, start, (spatial_rows, cot_rows))
    d_spatial = jnp.swapaxes(d_rows, 0, 1)

    def back_frame(carry, inputs):
        frame, d_frame = inputs
        act_in = jax.nn.silu(frame.astype(jnp.float32)).astype(jnp.bfloat16)
        padded = jnp.pad(act_in[None], edge)
        d_padded = jnp.pad(d_frame[None], edge)
        carry = carry + spatial_grad(padded, d_frame[None], row_count, col_count)
        d_act = conv_back(d_padded, w_spatial, row_count, col_count)[0]
        result = (d_frame.astype(jnp.float32) + silu_grad(frame.astype(jnp.float32)) * d_act).astype(jnp.bfloat16)
        return (carry, result)
    grad_space, grad_input = lax.scan(back_frame, jnp.zeros((3, 3, channels, channels), jnp.float32), (latents, d_spatial))
    factor = 1.0 / (latents.shape[0] * row_count * col_count) ** 0.5
    grad_time, grad_qkv, grad_out = grads_time
    return (grad_input, grad_space * factor, grad_time * factor, grad_qkv * factor, grad_out * factor)
```

```python
import math

import jax
import jax.numpy as jnp
from jax import lax
from jax.experimental import pallas as pl
from jax.experimental.pallas import tpu as pltpu
from jax.sharding import PartitionSpec as P

MESH = pl.DeviceIdType.MESH
BF = jnp.bfloat16
F32 = jnp.float32
HEADS = 8
C = 320
CP = 384
W = 106
WP = 112
ROWS = 2 * WP
UNIT = 128
GR = 1024
GL = 1024
NX, NY, NZ = 4, 4, 8


def nn(a, b):
    return lax.dot_general(a, b, (((1,), (0,)), ((), ())), preferred_element_type=F32)


def nt(a, b):
    return lax.dot_general(a, b, (((1,), (1,)), ((), ())), preferred_element_type=F32)


def tn(a, b):
    return lax.dot_general(a, b, (((0,), (0,)), ((), ())), preferred_element_type=F32)


def widen(x):
    return jnp.concatenate([x, jnp.zeros((x.shape[0], CP - C), x.dtype)], axis=1)


def pack3(a, b, c):
    b = pltpu.roll(b, 64, 1)
    return jnp.concatenate([a[:, :256], a[:, 256:] + b[:, :128], b[:, 128:], c], axis=1)


def silu_grad(v):
    sig = jax.nn.sigmoid(v)
    return sig * (1.0 + v * (1.0 - sig))


def up8(x):
    return jnp.concatenate([x[8:], jnp.zeros((8, x.shape[1]), x.dtype)], axis=0)


def down8(x):
    return jnp.concatenate([jnp.zeros((8, x.shape[1]), x.dtype), x[:-8]], axis=0)


def mega(
    seg, lat, cot, wsp_h, wt_h, wqkv_h, wout_h,
    gin, ft_out, fs_out,
    wsp, wt, wqkv, wq, wout, wo,
    latp, act, zbuf, snd_s, snd_c, rcv_s, rcv_c,
    u_act, u_dt, u_nrm, u_dq, u_mix, u_cot, snd_d, rcv_d,
    dp, dbuf, g_t, g_s, r0, r1, r2, r3, f_t, f_s, p1, p2, p3,
    wsem, hs, hr, a_s, a_r, dhs, dhr, s0s, s0r, s1s, s1r, s2s, s2r, s3s, s3r, osem,
):
    fr, row = lax.axis_index("frame"), lax.axis_index("row")
    y, core = fr // 2, fr % 2
    z, x = row // NX, row % NX
    nrow = NX * NZ

    def at(yy, cc, zz, xx):
        return {"frame": yy * 2 + cc, "row": zz * NX + xx}

    loads = [
        pltpu.make_async_copy(s, d, wsem.at[i])
        for i, (s, d) in enumerate([(wsp_h, wsp), (wt_h, wt), (wqkv_h, wqkv), (wout_h, wout)])
    ]
    for cp in loads:
        cp.start()

    def frame_peer(k):
        return {"frame": lax.rem(fr + k, 8), "row": row}

    def row_peer(k):
        return {"frame": fr, "row": lax.rem(row + k + nrow, nrow)}

    i1 = jnp.where(core == 0, x, y)
    i2 = jnp.where(core == 0, y, x)

    def first_peer(k):
        j = lax.rem(i1 + k, 4)
        return j, at(jnp.where(core == 0, y, j), core, z, jnp.where(core == 0, j, x))

    def second_peer(k):
        j = lax.rem(i2 + k, 4)
        return j, at(jnp.where(core == 0, j, y), core, z, jnp.where(core == 0, x, j))

    def z_peer(k):
        j = lax.rem(z + k, NZ)
        return j, at(y, core, j, x)

    sibling = at(y, 1 - core, z, x)

    barrier = pltpu.get_barrier_semaphore()
    peers = [frame_peer(k) for k in range(1, 8)]
    peers += [row_peer(1), row_peer(-1)]
    peers += [at(y, core, z, lax.rem(x + k, NX)) for k in range(1, NX)]
    peers += [z_peer(k)[1] for k in range(1, NZ)]
    for peer in peers:
        pl.semaphore_signal(barrier, inc=1, device_id=peer, device_id_type=MESH)

    def send(src, dst, ssem, rsem, peer):
        cp = pltpu.make_async_remote_copy(
            src_ref=src, dst_ref=dst, send_sem=ssem, recv_sem=rsem,
            device_id=peer, device_id_type=MESH,
        )
        cp.start()
        return cp

    latp[...] = jnp.zeros_like(latp)
    dp[...] = jnp.zeros_like(dp)
    for f in range(2):
        latp[f * WP : f * WP + W, :] = lat[f, 0].astype(F32)
        dp[f * WP : f * WP + W, :] = cot[f, 0].astype(F32)
    lv = latp[...]
    act[1] = (lv * jax.nn.sigmoid(lv)).astype(BF)

    def to_groups(src, dst):
        for g in range(16):
            if g < 14:
                t = jnp.concatenate(
                    [src[8 * g : 8 * g + 8, :], src[WP + 8 * g : WP + 8 * g + 8, :]], axis=0
                )
            else:
                t = jnp.zeros((16, C), F32)
            dst[g // 2, g % 2] = t.astype(BF)

    pl.semaphore_wait(barrier, len(peers))

    halo = [
        send(act.at[1], act.at[0], hs.at[0], hr.at[0], row_peer(1)),
        send(act.at[1], act.at[2], hs.at[1], hr.at[1], row_peer(-1)),
    ]

    def exchange(snd, rcv, ssem, rsem, base):
        cps = []
        for k in range(1, 8):
            cps.append(
                send(snd.at[lax.rem(fr + k, 8)], rcv.at[fr],
                     ssem.at[base + k - 1], rsem.at[base + k - 1], frame_peer(k))
            )
        rcv[pl.ds(fr, 1)] = snd[pl.ds(fr, 1)]
        return cps

    to_groups(dp, snd_c)
    cot_cps = exchange(snd_c, rcv_c, a_s, a_r, 0)

    for cp in loads:
        cp.wait()
    wo[...] = jnp.zeros_like(wo)
    wo[:C, :] = wout[...]
    for i in range(3):
        if i == 1:
            t = pltpu.roll(wqkv[:, 256:640].astype(F32), CP - 64, 1).astype(BF)
        else:
            t = wqkv[:, 640 * (i // 2) : 640 * (i // 2) + C]
        wq[i] = widen(t[:, :C])

    for cp in halo:
        cp.wait_recv()

    @pl.when(row == 0)
    def _():
        act[0] = jnp.zeros((ROWS, C), BF)

    @pl.when(row == nrow - 1)
    def _():
        act[2] = jnp.zeros((ROWS, C), BF)

    def conv_tap(b, carry):
        zbuf[b] = nn(act[0], wsp[0, b]) + nn(act[1], wsp[1, b]) + nn(act[2], wsp[2, b])
        return carry

    lax.fori_loop(0, 3, conv_tap, 0)
    rid = lax.broadcasted_iota(jnp.int32, (ROWS, C), 0)
    real = jnp.where(rid >= WP, rid - WP, rid) < W
    sp = latp[...] + pltpu.roll(zbuf[0], 1, 0) + zbuf[1] + pltpu.roll(zbuf[2], ROWS - 1, 0)
    zbuf[0] = jnp.where(real, sp, 0.0)
    to_groups(zbuf.at[0], snd_s)
    sp_cps = exchange(snd_s, rcv_s, a_s, a_r, 7)

    ri = lax.broadcasted_iota(jnp.int32, (UNIT, UNIT), 0)
    ci = lax.broadcasted_iota(jnp.int32, (UNIT, UNIT), 1)
    rseg = jnp.zeros((UNIT, UNIT), jnp.int32)
    cseg = jnp.zeros((UNIT, UNIT), jnp.int32)
    rid1 = lax.broadcasted_iota(jnp.int32, (UNIT, C), 0)
    nxt = jnp.zeros((UNIT, C), F32)
    prv = jnp.zeros((UNIT, C), F32)
    for f in range(16):
        rseg = jnp.where(ri // 8 == f, seg[f], rseg)
        cseg = jnp.where(ci // 8 == f, seg[f], cseg)
        if f < 15:
            ok = jnp.where(seg[f] == seg[f + 1], 1.0, 0.0).astype(F32)
            nxt = jnp.where(rid1 // 8 == f, ok, nxt)
            prv = jnp.where(rid1 // 8 == f + 1, ok, prv)
    bias = jnp.where((rseg == cseg) & (ri % 8 == ci % 8), 0.0, -1e30)
    scale = 1.0 / math.sqrt(C // HEADS)

    for cp in cot_cps:
        cp.wait_recv()
    for cp in sp_cps:
        cp.wait_recv()

    def unit(h, carry):
        spf = rcv_s[:, h].reshape(UNIT, C).astype(F32)
        cotb = rcv_c[:, h].reshape(UNIT, C)
        am = (spf * jax.nn.sigmoid(spf)).astype(BF)
        u_act[h] = am
        u_cot[h] = cotb
        tmp = spf + nn(am, wt[1])
        tmp = tmp + down8(nn(am, wt[0])) * prv
        tmp = tmp + up8(nn(am, wt[2])) * nxt
        tf = tmp.astype(BF).astype(F32)
        cen = tf - jnp.mean(tf, axis=-1, keepdims=True)
        inv = lax.rsqrt(jnp.mean(cen * cen, axis=-1, keepdims=True) + 1e-05)
        nhat = cen * inv
        nrm = nhat.astype(BF)
        u_nrm[h] = nrm
        q = nn(nrm, wq[0]).astype(BF)
        k = nn(nrm, wq[1]).astype(BF)
        v = nn(nrm, wq[2]).astype(BF)
        dm = nt(cotb, wo[...]).astype(BF)
        accs = [[None] * 3 for _ in range(4)]
        for hd in range(HEADS):
            lo, hi = 40 * hd, 40 * hd + 40
            t0, t1 = lo // 128, -(-hi // 128)
            w0, w1 = 128 * t0, 128 * t1
            lane = lax.broadcasted_iota(jnp.int32, (UNIT, w1 - w0), 1) + w0
            sel = (lane >= lo) & (lane < hi)

            def pick(t):
                return jnp.where(sel, t[:, w0:w1].astype(F32), 0.0).astype(BF)

            qm, km, vm, dmm = pick(q), pick(k), pick(v), pick(dm)
            s = nt(qm, km) * scale + bias
            e = jnp.exp(s - jnp.max(s, axis=-1, keepdims=True))
            p = e / jnp.sum(e, axis=-1, keepdims=True)
            pb = p.astype(BF)
            dpr = nt(dmm, vm)
            dsc = (p * (dpr - jnp.sum(p * dpr, axis=-1, keepdims=True)) * scale).astype(BF)
            for i, val in enumerate((nn(pb, vm), nn(dsc, km), tn(dsc, qm), tn(pb, dmm))):
                for t in range(t0, t1):
                    part = val[:, 128 * (t - t0) : 128 * (t - t0) + 128]
                    accs[i][t] = part if accs[i][t] is None else accs[i][t] + part
        mix, dq, dk, dv = (jnp.concatenate(a, axis=1) for a in accs)
        u_mix[h] = mix.astype(BF)
        dqkv = pack3(dq, dk, dv).astype(BF)
        u_dq[h] = dqkv
        dn = nt(dqkv[:, : 3 * C], wqkv[...])
        ln = inv * (
            dn
            - jnp.mean(dn, axis=-1, keepdims=True)
            - nhat * jnp.mean(dn * nhat, axis=-1, keepdims=True)
        )
        dt = (cotb.astype(F32) + ln).astype(BF)
        dtf = dt.astype(F32)
        u_dt[h] = pack3(widen(up8(dtf) * nxt), widen(dtf), widen(down8(dtf) * prv)).astype(BF)
        carried = nt(dt, wt[1]) + up8(nt(dt, wt[0])) * nxt + down8(nt(dt, wt[2])) * prv
        dsp = dtf + silu_grad(spf) * carried
        snd_d[:, h] = dsp.astype(BF).reshape(8, 16, C)
        return carry

    lax.fori_loop(0, 2, unit, 0)
    d_cps = exchange(snd_d, rcv_d, a_s, a_r, 14)

    g_t[...] = jnp.zeros_like(g_t)
    g_s[C * 3 :, :] = jnp.zeros((GR - C * 3, GL), BF)

    def both(ref):
        return jnp.concatenate([ref[0], ref[1]], axis=0)

    g_t[0:C, :] = tn(both(u_act), both(u_dt)).astype(BF)
    g_t[C : 2 * C, :] = tn(both(u_nrm), both(u_dq)).astype(BF)
    g_t[2 * C : 3 * C, 0:C] = tn(both(u_mix)[:, :C], both(u_cot)).astype(BF)

    half = GR // 2
    q1 = half // 4
    q2 = q1 // 4
    zl = GL // NZ
    mine = core * half
    other = (1 - core) * half
    base1 = mine + i1 * q1
    base2 = base1 + i2 * q2

    def r0_start(b, g):
        return [send(g.at[pl.ds(pl.multiple_of(other, 16), half)], r0.at[b],
                     s0s.at[b], s0r.at[b], sibling)]

    def r0_finish(b, g, cps):
        for cp in cps:
            cp.wait_recv()
        m = pl.ds(pl.multiple_of(mine, 16), half)
        p1[b] = (g[m, :].astype(F32) + r0[b].astype(F32)).astype(BF)

    def r1_start(b):
        cps = []
        for k in range(1, 4):
            j, peer = first_peer(k)
            cps.append(send(p1.at[b, pl.ds(pl.multiple_of(j * q1, 16), q1)], r1.at[b, k - 1],
                            s1s.at[b, k - 1], s1r.at[b, k - 1], peer))
        return cps

    def r1_finish(b, cps):
        for cp in cps:
            cp.wait_recv()
        t = p1[b, pl.ds(pl.multiple_of(i1 * q1, 16), q1), :].astype(F32)
        for k in range(3):
            t = t + r1[b, k].astype(F32)
        p2[b] = t.astype(BF)

    def r2_start(b):
        cps = []
        for k in range(1, 4):
            j, peer = second_peer(k)
            cps.append(send(p2.at[b, pl.ds(pl.multiple_of(j * q2, 16), q2)], r2.at[b, k - 1],
                            s2s.at[b, k - 1], s2r.at[b, k - 1], peer))
        return cps

    def r2_finish(b, cps):
        for cp in cps:
            cp.wait_recv()
        t = p2[b, pl.ds(pl.multiple_of(i2 * q2, 16), q2), :].astype(F32)
        for k in range(3):
            t = t + r2[b, k].astype(F32)
        t = t.astype(BF)
        for j in range(NZ):
            p3[b, j] = t[:, j * zl : (j + 1) * zl]

    def r3_start(b):
        cps = []
        for k in range(1, NZ):
            j, peer = z_peer(k)
            cps.append(send(p3.at[b, j], r3.at[b, k - 1], s3s.at[b, k - 1], s3r.at[b, k - 1], peer))
        return cps

    def r3_finish(b, f, cps):
        for cp in cps:
            cp.wait_recv()
        t = p3[b, z].astype(F32)
        for k in range(NZ - 1):
            t = t + r3[b, k].astype(F32)
        f[pl.ds(pl.multiple_of(base2, 16), q2), pl.ds(pl.multiple_of(z * zl, 128), zl)] = t.astype(BF)

    def g3_start(b, f):
        piece = f.at[pl.ds(pl.multiple_of(base2, 16), q2), pl.ds(pl.multiple_of(z * zl, 128), zl)]
        return [send(piece, piece, s3s.at[b + 2, k - 1], s3r.at[b + 2, k - 1], z_peer(k)[1])
                for k in range(1, NZ)]

    def g2_start(b, f):
        piece = f.at[pl.ds(pl.multiple_of(base2, 16), q2)]
        return [send(piece, piece, s2s.at[b + 2, k - 1], s2r.at[b + 2, k - 1], second_peer(k)[1])
                for k in range(1, 4)]

    def g1_start(b, f):
        piece = f.at[pl.ds(pl.multiple_of(base1, 16), q1)]
        return [send(piece, piece, s1s.at[b + 2, k - 1], s1r.at[b + 2, k - 1], first_peer(k)[1])
                for k in range(1, 4)]

    def g0_start(b, f):
        piece = f.at[pl.ds(pl.multiple_of(mine, 16), half)]
        return [send(piece, piece, s0s.at[b + 2], s0r.at[b + 2], sibling)]

    done = []
    t0c = r0_start(0, g_t)

    for cp in d_cps:
        cp.wait_recv()
    for g in range(14):
        t = rcv_d[g // 2, g % 2].astype(F32)
        dp[8 * g : 8 * g + 8, :] = t[:8]
        dp[WP + 8 * g : WP + 8 * g + 8, :] = t[8:]
    dv = dp[...]
    dbuf[1] = dv.astype(BF)
    dhalo = [
        send(dbuf.at[1], dbuf.at[0], dhs.at[0], dhr.at[0], row_peer(1)),
        send(dbuf.at[1], dbuf.at[2], dhs.at[1], dhr.at[1], row_peer(-1)),
    ]
    dcat = pack3(
        widen(pltpu.roll(dv, ROWS - 1, 0)), widen(dv), widen(pltpu.roll(dv, 1, 0))
    ).astype(BF)
    for a in range(3):
        g_s[a * C : (a + 1) * C, :] = tn(act[a], dcat).astype(BF)
    s0c = r0_start(1, g_s)
    r0_finish(0, g_t, t0c)
    t1c = r1_start(0)
    r0_finish(1, g_s, s0c)
    s1c = r1_start(1)

    for cp in dhalo:
        cp.wait_recv()

    @pl.when(row == 0)
    def _():
        dbuf[0] = jnp.zeros((ROWS, C), BF)

    @pl.when(row == nrow - 1)
    def _():
        dbuf[2] = jnp.zeros((ROWS, C), BF)

    def back_tap(b, carry):
        zbuf[b] = nt(dbuf[2], wsp[0, b]) + nt(dbuf[1], wsp[1, b]) + nt(dbuf[0], wsp[2, b])
        return carry

    lax.fori_loop(0, 3, back_tap, 0)
    da = pltpu.roll(zbuf[0], ROWS - 1, 0) + zbuf[1] + pltpu.roll(zbuf[2], 1, 0)
    dp[...] = dp[...] + silu_grad(latp[...]) * da
    for f in range(2):
        gin[f, 0] = dp[f * WP : f * WP + W, :].astype(BF)

    r1_finish(0, t1c)
    t2c = r2_start(0)
    r1_finish(1, s1c)
    s2c = r2_start(1)
    r2_finish(0, t2c)
    t3c = r3_start(0)
    r2_finish(1, s2c)
    s3c = r3_start(1)
    r3_finish(0, f_t, t3c)
    tg = g3_start(0, f_t)
    r3_finish(1, f_s, s3c)
    sg = g3_start(1, f_s)
    done += t0c + s0c + t1c + s1c + t2c + s2c + t3c + s3c
    for start in (g2_start, g1_start, g0_start):
        for cp in tg:
            cp.wait_recv()
        done += tg
        tg = start(0, f_t)
        for cp in sg:
            cp.wait_recv()
        done += sg
        sg = start(1, f_s)
    done += tg + sg
    outs = []
    for cps, f, o, i in ((tg, f_t, ft_out, 0), (sg, f_s, fs_out, 1)):
        for cp in cps:
            cp.wait_recv()
        cp = pltpu.make_async_copy(f, o, osem.at[i])
        cp.start()
        outs.append(cp)
    for cp in halo + cot_cps + sp_cps + d_cps + dhalo + done:
        cp.wait_send()
    for cp in outs:
        cp.wait()


def unpack(ref, r0, r1, factor):
    x = ref[r0:r1, :].astype(F32) * factor
    return x[:, :C], pltpu.roll(x[:, 256:640], CP - 64, 1)[:, :C], x[:, 640 : 640 + C]


def finish(factor, ft, fs, gs, gt, gq, go):
    for a in range(3):
        for b, t in enumerate(unpack(fs, a * C, (a + 1) * C, factor)):
            gs[a, b] = t
    for b, t in enumerate(unpack(ft, 0, C, factor)):
        gt[b] = t
    gq[...] = (ft[C : 2 * C, :].astype(F32) * factor)[:, : 3 * C]
    go[...] = (ft[2 * C : 3 * C, :].astype(F32) * factor)[:, :C]


def on_device(latents, segments, w_spatial, w_temporal, w_qkv, w_out, cotangent):
    vm = pl.BlockSpec(memory_space=pltpu.VMEM)
    anyspec = pl.BlockSpec(memory_space=pl.ANY)
    dma = pltpu.SemaphoreType.DMA
    V = pltpu.VMEM
    gin, ft, fs = pl.pallas_call(
        mega,
        out_shape=(
            jax.ShapeDtypeStruct(latents.shape, BF),
            jax.ShapeDtypeStruct((GR, GL), BF),
            jax.ShapeDtypeStruct((GR, GL), BF),
        ),
        in_specs=[pl.BlockSpec(memory_space=pltpu.SMEM), vm, vm] + [anyspec] * 4,
        out_specs=(vm, anyspec, anyspec),
        scratch_shapes=[
            V((3, 3, C, C), BF), V((3, C, C), BF), V((C, 3 * C), BF), V((3, C, CP), BF),
            V((C, C), BF), V((CP, C), BF),
            V((ROWS, C), F32), V((3, ROWS, C), BF), V((3, ROWS, C), F32),
            V((8, 2, 16, C), BF), V((8, 2, 16, C), BF), V((8, 2, 16, C), BF), V((8, 2, 16, C), BF),
            V((2, UNIT, C), BF), V((2, UNIT, GL), BF), V((2, UNIT, C), BF), V((2, UNIT, GL), BF),
            V((2, UNIT, CP), BF), V((2, UNIT, C), BF),
            V((8, 2, 16, C), BF), V((8, 2, 16, C), BF),
            V((ROWS, C), F32), V((3, ROWS, C), BF),
            V((GR, GL), BF), V((GR, GL), BF),
            V((2, GR // 2, GL), BF), V((2, 3, GR // 8, GL), BF), V((2, 3, GR // 32, GL), BF),
            V((2, NZ - 1, GR // 32, GL // NZ), BF),
            V((GR, GL), BF), V((GR, GL), BF),
            V((2, GR // 2, GL), BF), V((2, GR // 8, GL), BF), V((2, NZ, GR // 32, GL // NZ), BF),
            dma((4,)), dma((2,)), dma((2,)), dma((21,)), dma((21,)), dma((2,)), dma((2,)),
            dma((4,)), dma((4,)), dma((4, 3)), dma((4, 3)), dma((4, 3)), dma((4, 3)),
            dma((4, NZ - 1)), dma((4, NZ - 1)), dma((2,)),
        ],
        compiler_params=pltpu.CompilerParams(
            collective_id=0, has_side_effects=True, vmem_limit_bytes=56 * 1024 * 1024
        ),
        name="mega",
    )(segments, latents, cotangent, w_spatial, w_temporal, w_qkv, w_out)
    factor = 1.0 / math.sqrt(54272)
    gs, gt, gq, go = pl.pallas_call(
        lambda *refs: finish(factor, *refs),
        out_shape=(
            jax.ShapeDtypeStruct((3, 3, C, C), F32),
            jax.ShapeDtypeStruct((3, C, C), F32),
            jax.ShapeDtypeStruct((C, 3 * C), F32),
            jax.ShapeDtypeStruct((C, C), F32),
        ),
        in_specs=[vm] * 2,
        out_specs=(vm,) * 4,
        compiler_params=pltpu.CompilerParams(vmem_limit_bytes=56 * 1024 * 1024),
        name="finish",
    )(ft, fs)
    return gin, gs, gt, gq, go


def solution(mesh):
    in_specs = (
        P("frame", "row", None, None),
        P(),
        P(),
        P(),
        P(),
        P(),
        P("frame", "row", None, None),
    )
    out_specs = (P("frame", "row", None, None), P(), P(), P(), P())
    return jax.shard_map(
        on_device, mesh=mesh, in_specs=in_specs, out_specs=out_specs, check_vma=False
    )
```

```python
import math

import jax
import jax.numpy as jnp
from jax import lax
from jax.experimental import pallas as pl
from jax.experimental.pallas import tpu as pltpu
from jax.sharding import PartitionSpec as P

MESH = pl.DeviceIdType.MESH
BF = jnp.bfloat16
F32 = jnp.float32
HEADS = 8
C = 320
CP = 384
W = 106
WP = 112
ROWS = 2 * WP
UNIT = 128
NR = (768, 960)
GL = 1024
NX, NY, NZ = 4, 4, 8


def nn(a, b):
    return lax.dot_general(a, b, (((1,), (0,)), ((), ())), preferred_element_type=F32)


def nt(a, b):
    return lax.dot_general(a, b, (((1,), (1,)), ((), ())), preferred_element_type=F32)


def tn(a, b):
    return lax.dot_general(a, b, (((0,), (0,)), ((), ())), preferred_element_type=F32)


def widen(x):
    return jnp.concatenate([x, jnp.zeros((x.shape[0], CP - C), x.dtype)], axis=1)


def pack3(a, b, c):
    b = pltpu.roll(b, 64, 1)
    return jnp.concatenate([a[:, :256], a[:, 256:] + b[:, :128], b[:, 128:], c], axis=1)


def silu_grad(v):
    sig = jax.nn.sigmoid(v)
    return sig * (1.0 + v * (1.0 - sig))


def up8(x):
    return jnp.concatenate([x[8:], jnp.zeros((8, x.shape[1]), x.dtype)], axis=0)


def down8(x):
    return jnp.concatenate([jnp.zeros((8, x.shape[1]), x.dtype), x[:-8]], axis=0)


OUT_BLOCKS = (
    [(640, 256 * j + 128 * r, 128 * r, 128 * j, 128) for j in range(3) for r in range(2)]
    + [(640, 768, 256, 0, 64), (704, 768, 256, 128, 64), (640, 896, 256, 256, 64)]
)


def mega(
    seg_h, lat, cot, wsp_h, wt_h, wqkv_h, wout_h,
    gi, f_t, f_s,
    seg, wsp, wt, wqkv, wq, wtr, wout, wo,
    latn, latp, act, zbuf, snd_s, snd_c, rcv_s, rcv_c,
    u_act, u_dt, u_nrm, u_dq, u_mix, u_cot, snd_d, rcv_d,
    dp, dbuf, g_t, g_s, r0, r1, r2, r3, p1, p2, p3, g3,
    wsem, hs, hr, a_s, a_r, dhs, dhr, s0s, s0r, s1s, s1r, s2s, s2r, s3s, s3r,
):
    fr, row = lax.axis_index("frame"), lax.axis_index("row")
    y, core = fr // 2, fr % 2
    z, x = row // NX, row % NX
    nrow = NX * NZ

    def at(yy, cc, zz, xx):
        return {"frame": yy * 2 + cc, "row": zz * NX + xx}

    def frame_peer(k):
        return {"frame": lax.rem(fr + k, 8), "row": row}

    def row_peer(k):
        return {"frame": fr, "row": lax.rem(row + k + nrow, nrow)}

    i1 = jnp.where(core == 0, x, y)
    i2 = jnp.where(core == 0, y, x)

    def first_peer(k):
        j = lax.rem(i1 + k, 4)
        return j, at(jnp.where(core == 0, y, j), core, z, jnp.where(core == 0, j, x))

    def second_peer(k):
        j = lax.rem(i2 + k, 4)
        return j, at(jnp.where(core == 0, j, y), core, z, jnp.where(core == 0, x, j))

    def z_peer(k):
        j = lax.rem(z + k, NZ)
        return j, at(y, core, j, x)

    sibling = at(y, 1 - core, z, x)

    barrier = pltpu.get_barrier_semaphore()
    peers = [z_peer(k)[1] for k in range(1, NZ)]
    peers += [frame_peer(k) for k in range(1, 8)]
    peers += [row_peer(1), row_peer(-1)]
    peers += [at(y, core, z, lax.rem(x + k, NX)) for k in range(1, NX)]
    for peer in peers:
        pl.semaphore_signal(barrier, inc=1, device_id=peer, device_id_type=MESH)

    loads = [
        pltpu.make_async_copy(s, d, wsem.at[i])
        for i, (s, d) in enumerate(
            [(lat, latn.at[0]), (cot, latn.at[1]), (wqkv_h, wqkv), (wout_h, wout), (wsp_h, wsp), (wt_h, wt), (seg_h, seg)]
        )
    ]
    for cp in loads:
        cp.start()

    def send(src, dst, ssem, rsem, peer):
        cp = pltpu.make_async_remote_copy(
            src_ref=src, dst_ref=dst, send_sem=ssem, recv_sem=rsem,
            device_id=peer, device_id_type=MESH,
        )
        cp.start()
        return cp

    latp[...] = jnp.zeros_like(latp)
    dp[...] = jnp.zeros_like(dp)

    def rows_of(i, dst):
        loads[i].wait()
        v = latn[i].astype(F32)
        for f in range(2):
            dst[f * WP : f * WP + W, :] = v[:, f, :]

    rows_of(0, latp)
    lv = latp[...]
    act[1] = (lv * jax.nn.sigmoid(lv)).astype(BF)

    def to_groups(src, dst):
        for g in range(16):
            if g < 14:
                t = jnp.concatenate(
                    [src[8 * g : 8 * g + 8, :], src[WP + 8 * g : WP + 8 * g + 8, :]], axis=0
                )
            else:
                t = jnp.zeros((16, C), F32)
            dst[g // 2, g % 2] = t.astype(BF)

    pl.semaphore_wait(barrier, len(peers))

    halo = [
        send(act.at[1], act.at[0], hs.at[0], hr.at[0], row_peer(1)),
        send(act.at[1], act.at[2], hs.at[1], hr.at[1], row_peer(-1)),
    ]

    def exchange(snd, rcv, ssem, rsem, base):
        cps = []
        for k in range(1, 8):
            cps.append(
                send(snd.at[lax.rem(fr + k, 8)], rcv.at[fr],
                     ssem.at[base + k - 1], rsem.at[base + k - 1], frame_peer(k))
            )
        rcv[pl.ds(fr, 1)] = snd[pl.ds(fr, 1)]
        return cps

    rows_of(1, dp)
    to_groups(dp, snd_c)
    cot_cps = exchange(snd_c, rcv_c, a_s, a_r, 0)

    for cp in loads[2:]:
        cp.wait()
    wo[...] = jnp.zeros_like(wo)
    wo[:C, :] = wout[...]
    for i in range(3):
        if i == 1:
            t = pltpu.roll(wqkv[:, 256:640].astype(F32), CP - 64, 1).astype(BF)
        else:
            t = wqkv[:, 640 * (i // 2) : 640 * (i // 2) + C]
        t = widen(t[:, :C])
        wq[i] = t
        if i > 0:
            wtr[i - 1] = t.T

    ri = lax.broadcasted_iota(jnp.int32, (UNIT, UNIT), 0)
    ci = lax.broadcasted_iota(jnp.int32, (UNIT, UNIT), 1)
    rseg = jnp.zeros((UNIT, UNIT), jnp.int32)
    cseg = jnp.zeros((UNIT, UNIT), jnp.int32)
    nxt = jnp.zeros((UNIT, UNIT), F32)
    prv = jnp.zeros((UNIT, UNIT), F32)
    for f in range(16):
        rseg = jnp.where(ri // 8 == f, seg[f], rseg)
        cseg = jnp.where(ci // 8 == f, seg[f], cseg)
        if f < 15:
            ok = jnp.where(seg[f] == seg[f + 1], 1.0, 0.0).astype(F32)
            nxt = jnp.where(ri // 8 == f, ok, nxt)
            prv = jnp.where(ri // 8 == f + 1, ok, prv)
    bias = jnp.where((rseg == cseg) & (ri % 8 == ci % 8), 0.0, -1e30)

    def wide(m):
        m = jnp.concatenate([m, m, m], axis=1)[:, :C]
        return jnp.concatenate([m, m], axis=0)

    nxt, prv = wide(nxt), wide(prv)
    scale = 1.0 / math.sqrt(C // HEADS)

    for cp in halo:
        cp.wait_recv()

    @pl.when(row == 0)
    def _():
        act[0] = jnp.zeros((ROWS, C), BF)

    @pl.when(row == nrow - 1)
    def _():
        act[2] = jnp.zeros((ROWS, C), BF)

    for b in range(3):
        zbuf[b] = nn(act[0], wsp[0, b]) + nn(act[1], wsp[1, b]) + nn(act[2], wsp[2, b])
    rid = lax.broadcasted_iota(jnp.int32, (ROWS, C), 0)
    real = jnp.where(rid >= WP, rid - WP, rid) < W
    sp = latp[...] + pltpu.roll(zbuf[0], 1, 0) + zbuf[1] + pltpu.roll(zbuf[2], ROWS - 1, 0)
    zbuf[0] = jnp.where(real, sp, 0.0)
    to_groups(zbuf.at[0], snd_s)
    sp_cps = exchange(snd_s, rcv_s, a_s, a_r, 7)

    for cp in cot_cps:
        cp.wait_recv()
    for cp in sp_cps:
        cp.wait_recv()

    def both(ref):
        return jnp.concatenate([ref[:, h].reshape(UNIT, C) for h in range(2)], axis=0)

    spf = both(rcv_s).astype(F32)
    cotb = both(rcv_c)
    am = (spf * jax.nn.sigmoid(spf)).astype(BF)
    u_act[...] = am
    u_cot[...] = cotb
    tmp = spf + nn(am, wt[1])
    tmp = tmp + down8(nn(am, wt[0])) * prv
    tmp = tmp + up8(nn(am, wt[2])) * nxt
    tf = tmp.astype(BF).astype(F32)
    cen = tf - jnp.mean(tf, axis=-1, keepdims=True)
    inv = lax.rsqrt(jnp.mean(cen * cen, axis=-1, keepdims=True) + 1e-05)
    nhat = cen * inv
    nrm = nhat.astype(BF)
    u_nrm[...] = nrm
    qall = nn(nrm, wq[0]).astype(BF)
    kall = nn(nrm, wq[1]).astype(BF)
    vall = nn(nrm, wq[2]).astype(BF)
    kt = nt(wtr[0], nrm)
    vt = nt(wtr[1], nrm)
    dmall = nt(cotb, wo[...]).astype(BF)

    def attention(u):
        rows = slice(UNIT * u, UNIT * u + UNIT)
        state, mixt, dqt = [], [], []
        dk, dv = [None] * 3, [None] * 3
        for hd in range(HEADS):
            lo, hi = 40 * hd, 40 * hd + 40
            t0, t1 = lo // 128, -(-hi // 128)
            w0, w1 = 128 * t0, 128 * t1
            lane = lax.broadcasted_iota(jnp.int32, (UNIT, w1 - w0), 1) + w0
            sel = (lane >= lo) & (lane < hi)
            qm = jnp.where(sel, qall[rows, w0:w1].astype(F32), 0.0).astype(BF)
            dmm = jnp.where(sel, dmall[rows, w0:w1].astype(F32), 0.0).astype(BF)
            state.append((lo, hi, t0, t1, qm, dmm, nt(kall[rows, w0:w1], qm), nt(vall[rows, w0:w1], dmm)))
        second = []
        for lo, hi, t0, t1, qm, dmm, s, dpr in state:
            s = s * scale + bias
            e = jnp.exp(s - jnp.max(s, axis=0, keepdims=True))
            p = e * (1.0 / jnp.sum(e, axis=0, keepdims=True))
            ds = (p * (dpr - jnp.sum(p * dpr, axis=0, keepdims=True)) * scale).astype(BF)
            second.append((lo, hi, t0, t1, qm, dmm, p.astype(BF), ds))
        for lo, hi, t0, t1, qm, dmm, pb, ds in second:
            mixt.append(nn(vt[lo:hi, rows].astype(BF), pb))
            dqt.append(nn(kt[lo:hi, rows].astype(BF), ds))
            for acc, val in ((dk, nn(ds, qm)), (dv, nn(pb, dmm))):
                for t in range(t0, t1):
                    part = val[:, 128 * (t - t0) : 128 * (t - t0) + 128]
                    acc[t] = part if acc[t] is None else acc[t] + part
        u_mix[:, rows] = jnp.concatenate(mixt, axis=0).astype(BF)
        dq = widen(jnp.concatenate(dqt, axis=0).T)
        u_dq[rows, :] = pack3(dq, jnp.concatenate(dk, axis=1), jnp.concatenate(dv, axis=1)).astype(BF)

    attention(0)
    attention(1)
    dn = nt(u_dq[:, : 3 * C], wqkv[...])
    ln = inv * (
        dn
        - jnp.mean(dn, axis=-1, keepdims=True)
        - nhat * jnp.mean(dn * nhat, axis=-1, keepdims=True)
    )
    dt = (cotb.astype(F32) + ln).astype(BF)
    dtf = dt.astype(F32)
    carried = nt(dt, wt[1]) + up8(nt(dt, wt[0])) * nxt + down8(nt(dt, wt[2])) * prv
    dsp = (dtf + silu_grad(spf) * carried).astype(BF)
    for h in range(2):
        snd_d[:, h] = dsp[UNIT * h : UNIT * h + UNIT].reshape(8, 16, C)
    d_cps = exchange(snd_d, rcv_d, a_s, a_r, 14)

    u_dt[...] = pack3(widen(up8(dtf) * nxt), widen(dtf), widen(down8(dtf) * prv)).astype(BF)
    g_t[0:C, :] = tn(u_act[...], u_dt[...]).astype(BF)
    g_t[C : 2 * C, :] = tn(u_nrm[...], u_dq[...]).astype(BF)
    go = widen(nn(u_mix[...], u_cot[...])).astype(BF)
    g_t[2 * C : 2 * C + 128, 768:] = jnp.zeros((128, 256), BF)
    for dst, lane, src, col, n in OUT_BLOCKS:
        g_t[dst : dst + n, lane : lane + 128] = go[src : src + n, col : col + 128]

    bufs = (g_t, g_s)
    outs = (f_t, f_s)
    half = [n // 2 for n in NR]
    quar = [n // 4 for n in NR]
    mine = [pl.multiple_of(core * n, 16) for n in half]
    other = [pl.multiple_of((1 - core) * n, 16) for n in half]
    low = [pl.multiple_of(i2 // 2 * n, 16) for n in quar]
    lane1 = pl.multiple_of(i1 * 256, 256)
    lane2 = pl.multiple_of(i2 % 2 * 128, 128)

    def r0_start(b):
        return [
            send(bufs[b].at[pl.ds(other[b], half[b]), pl.ds(256 * j, 256)],
                 r0.at[b, pl.ds(0, half[b]), pl.ds(256 * j, 256)], s0s.at[b, j], s0r.at[b, j], sibling)
            for j in range(4)
        ]

    def r0_finish(b, cps):
        for j, cp in enumerate(cps):
            cp.wait_recv()
            sl = slice(256 * j, 256 * j + 256)
            p1[b, : half[b], sl] = (
                bufs[b][pl.ds(mine[b], half[b]), sl].astype(F32) + r0[b, : half[b], sl].astype(F32)
            ).astype(BF)

    def r1_start(b):
        cps = []
        for k in range(1, 4):
            j, peer = first_peer(k)
            cps.append(
                send(p1.at[b, pl.ds(0, half[b]), pl.ds(pl.multiple_of(j * 256, 256), 256)],
                     r1.at[b, k - 1, pl.ds(0, half[b])], s1s.at[b, k - 1], s1r.at[b, k - 1], peer)
            )
        return cps

    def r1_finish(b, cps):
        for cp in cps:
            cp.wait_recv()
        t = p1[b, : half[b], pl.ds(lane1, 256)].astype(F32)
        for k in range(3):
            t = t + r1[b, k, : half[b]].astype(F32)
        p2[b, : half[b]] = t.astype(BF)

    def r2_start(b):
        cps = []
        for k in range(1, 4):
            j, peer = second_peer(k)
            cps.append(
                send(p2.at[b, pl.ds(pl.multiple_of(j // 2 * quar[b], 16), quar[b]),
                           pl.ds(pl.multiple_of(j % 2 * 128, 128), 128)],
                     r2.at[b, k - 1, pl.ds(0, quar[b])], s2s.at[b, k - 1], s2r.at[b, k - 1], peer)
            )
        return cps

    def r2_finish(b, cps):
        for cp in cps:
            cp.wait_recv()
        t = p2[b, pl.ds(low[b], quar[b]), pl.ds(lane2, 128)].astype(F32)
        for k in range(3):
            t = t + r2[b, k, : quar[b]].astype(F32)
        p3[b, : quar[b]] = t.astype(BF)
        p3[b, quar[b] :] = jnp.zeros((256 - quar[b], 128), BF)

    def r3_start(b):
        cps = []
        for k in range(1, NZ):
            j, peer = z_peer(k)
            cps.append(
                send(p3.at[b, pl.ds(pl.multiple_of(j * 32, 32), 32)], r3.at[b, k - 1],
                     s3s.at[b, k - 1], s3r.at[b, k - 1], peer)
            )
        return cps

    zrow = pl.multiple_of(z * 32, 32)

    def r3_finish(b, cps):
        for cp in cps:
            cp.wait_recv()
        t = p3[b, pl.ds(zrow, 32)].astype(F32)
        for k in range(NZ - 1):
            t = t + r3[b, k].astype(F32)
        g3[b, pl.ds(zrow, 32)] = t.astype(BF)

    def g3_start(b):
        piece = g3.at[b, pl.ds(zrow, 32)]
        return [
            send(piece, piece, s3s.at[b + 2, k - 1], s3r.at[b + 2, k - 1], z_peer(k)[1])
            for k in range(1, NZ)
        ]

    def g3_finish(b, cps):
        for cp in cps:
            cp.wait_recv()
        outs[b][pl.ds(pl.multiple_of(mine[b] + low[b], 16), quar[b]),
                pl.ds(pl.multiple_of(lane1 + lane2, 128), 128)] = g3[b, : quar[b]]

    def g2_start(b):
        piece = outs[b].at[pl.ds(pl.multiple_of(mine[b] + low[b], 16), quar[b]),
                           pl.ds(pl.multiple_of(lane1 + lane2, 128), 128)]
        return [
            send(piece, piece, s2s.at[b + 2, k - 1], s2r.at[b + 2, k - 1], second_peer(k)[1])
            for k in range(1, 4)
        ]

    def block(b, j):
        return outs[b].at[pl.ds(mine[b], half[b]), pl.ds(pl.multiple_of(j * 256, 256), 256)]

    def g1_start(b):
        piece = block(b, i1)
        return [
            send(piece, piece, s1s.at[b + 2, k - 1], s1r.at[b + 2, k - 1], first_peer(k)[1])
            for k in range(1, 4)
        ]

    def g0_start(b, k):
        piece = block(b, lax.rem(i1 - k + 4, 4))
        return send(piece, piece, s0s.at[b + 2, k], s0r.at[b + 2, k], sibling)

    def got(cps):
        for cp in cps:
            cp.wait_recv()

    sent = []

    def keep(cps):
        sent.extend(cps)
        return cps

    t0c = keep(r0_start(0))
    r0_finish(0, t0c)
    t1c = keep(r1_start(0))

    got(d_cps)
    for g in range(14):
        t = rcv_d[g // 2, g % 2].astype(F32)
        dp[8 * g : 8 * g + 8, :] = t[:8]
        dp[WP + 8 * g : WP + 8 * g + 8, :] = t[8:]
    dv = dp[...]
    dbuf[1] = dv.astype(BF)
    dcat = pack3(
        widen(pltpu.roll(dv, ROWS - 1, 0)), widen(dv), widen(pltpu.roll(dv, 1, 0))
    ).astype(BF)
    for a in range(3):
        g_s[a * C : (a + 1) * C, :] = tn(act[a], dcat).astype(BF)
    s0c = keep(r0_start(1))
    r0_finish(1, s0c)
    s1c = keep(r1_start(1))
    dhalo = [
        send(dbuf.at[1], dbuf.at[0], dhs.at[0], dhr.at[0], row_peer(1)),
        send(dbuf.at[1], dbuf.at[2], dhs.at[1], dhr.at[1], row_peer(-1)),
    ]
    r1_finish(0, t1c)
    t2c = keep(r2_start(0))
    r2_finish(0, t2c)
    t3c = keep(r3_start(0))
    r1_finish(1, s1c)
    s2c = keep(r2_start(1))
    r3_finish(0, t3c)
    t4c = keep(g3_start(0))
    r2_finish(1, s2c)
    s3c = keep(r3_start(1))

    got(dhalo)

    @pl.when(row == 0)
    def _():
        dbuf[0] = jnp.zeros((ROWS, C), BF)

    @pl.when(row == nrow - 1)
    def _():
        dbuf[2] = jnp.zeros((ROWS, C), BF)

    for b in range(3):
        zbuf[b] = nt(dbuf[2], wsp[0, b]) + nt(dbuf[1], wsp[1, b]) + nt(dbuf[0], wsp[2, b])
    da = pltpu.roll(zbuf[0], ROWS - 1, 0) + zbuf[1] + pltpu.roll(zbuf[2], 1, 0)
    gi[...] = (dp[...] + silu_grad(latp[...]) * da).astype(BF)

    g3_finish(0, t4c)
    t5c = keep(g2_start(0))
    r3_finish(1, s3c)
    s4c = keep(g3_start(1))
    got(t5c)
    t6c = keep(g1_start(0))
    g3_finish(1, s4c)
    s5c = keep(g2_start(1))
    got(s5c)
    s6c = keep(g1_start(1))
    s7c = [g0_start(1, 0)]
    t7c = [g0_start(0, 0)]
    for k in range(1, 4):
        t6c[k - 1].wait_recv()
        t7c.append(g0_start(0, k))
    for k in range(1, 4):
        s6c[k - 1].wait_recv()
        s7c.append(g0_start(1, k))
    keep(t7c + s7c)
    got(t7c)
    got(s7c)
    for cp in halo + cot_cps + sp_cps + d_cps + dhalo + sent:
        cp.wait_send()


def unpack(x):
    return x[:, :C], pltpu.roll(x[:, 256:640], CP - 64, 1)[:, :C], x[:, 640 : 640 + C]


def finish(factor, gi, ft, fs, gin, gs, gt, gq, go, vs, vt, vq, vo, vi, sem):
    cps = []

    def out(src, dst):
        cp = pltpu.make_async_copy(src, dst, sem.at[len(cps)])
        cp.start()
        cps.append(cp)

    for a in range(3):
        for b, t in enumerate(unpack(fs[a * C : (a + 1) * C, :].astype(F32) * factor)):
            vs[a, b] = t
        out(vs.at[a], gs.at[a])
    for b, t in enumerate(unpack(ft[0:C, :].astype(F32) * factor)):
        vt[b] = t
    out(vt, gt)
    vq[...] = (ft[C : 2 * C, :].astype(F32) * factor)[:, : 3 * C]
    out(vq, gq)
    for dst, lane, src, col, n in OUT_BLOCKS:
        w = min(128, C - col)
        vo[src : src + n, col : col + w] = ft[dst : dst + n, lane : lane + w].astype(F32) * factor
    out(vo, go)
    g = gi[...].astype(F32)
    vi[...] = jnp.stack([g[:W], g[WP : WP + W]], axis=1).astype(BF)
    out(vi, gin)
    for cp in cps:
        cp.wait()


def on_device(latents, segments, w_spatial, w_temporal, w_qkv, w_out, cotangent):
    vm = pl.BlockSpec(memory_space=pltpu.VMEM)
    anyspec = pl.BlockSpec(memory_space=pl.ANY)
    dma = pltpu.SemaphoreType.DMA
    V = pltpu.VMEM
    hm, qm = max(NR) // 2, max(NR) // 4

    def by_column(t):
        return jnp.transpose(t.reshape(2, W, C), (1, 0, 2))

    gi, ft, fs = pl.pallas_call(
        mega,
        out_shape=(
            jax.ShapeDtypeStruct((ROWS, C), BF),
            jax.ShapeDtypeStruct((NR[0], GL), BF),
            jax.ShapeDtypeStruct((NR[1], GL), BF),
        ),
        in_specs=[pl.BlockSpec(memory_space=pltpu.HBM)] * 7,
        out_specs=(vm, vm, vm),
        scratch_shapes=[
            pltpu.SMEM((16,), jnp.int32), V((3, 3, C, C), BF), V((3, C, C), BF), V((C, 3 * C), BF), V((3, C, CP), BF),
            V((2, CP, C), BF), V((C, C), BF), V((CP, C), BF),
            V((2, W, 2, C), BF), V((ROWS, C), F32), V((3, ROWS, C), BF), V((3, ROWS, C), F32),
            V((8, 2, 16, C), BF), V((8, 2, 16, C), BF), V((8, 2, 16, C), BF), V((8, 2, 16, C), BF),
            V((2 * UNIT, C), BF), V((2 * UNIT, GL), BF), V((2 * UNIT, C), BF), V((2 * UNIT, GL), BF),
            V((C, 2 * UNIT), BF), V((2 * UNIT, C), BF),
            V((8, 2, 16, C), BF), V((8, 2, 16, C), BF),
            V((ROWS, C), F32), V((3, ROWS, C), BF),
            V((NR[0], GL), BF), V((NR[1], GL), BF),
            V((2, hm, GL), BF), V((2, 3, hm, 256), BF), V((2, 3, qm, 128), BF),
            V((2, NZ - 1, 32, 128), BF),
            V((2, hm, GL), BF), V((2, hm, 256), BF), V((2, 256, 128), BF), V((2, 256, 128), BF),
            dma((7,)), dma((2,)), dma((2,)), dma((21,)), dma((21,)), dma((2,)), dma((2,)),
            dma((4, 4)), dma((4, 4)), dma((4, 3)), dma((4, 3)), dma((4, 3)), dma((4, 3)),
            dma((4, NZ - 1)), dma((4, NZ - 1)),
        ],
        compiler_params=pltpu.CompilerParams(
            collective_id=0, has_side_effects=True, vmem_limit_bytes=40 * 1024 * 1024
        ),
        name="mega",
    )(*(
        pltpu.with_memory_space_constraint(t, pltpu.HBM)
        for t in (segments, by_column(latents), by_column(cotangent), w_spatial, w_temporal, w_qkv, w_out)
    ))
    factor = 1.0 / math.sqrt(54272)
    shapes = [(3, 3, C, C), (3, C, C), (C, 3 * C), (C, C)]
    gin, gs, gt, gq, go = pl.pallas_call(
        lambda *refs: finish(factor, *refs),
        out_shape=(jax.ShapeDtypeStruct((W, 2, C), BF),)
        + tuple(jax.ShapeDtypeStruct(s, F32) for s in shapes),
        in_specs=[vm] * 3,
        out_specs=(anyspec,) * 5,
        scratch_shapes=[V(s, F32) for s in shapes] + [V((W, 2, C), BF), dma((7,))],
        compiler_params=pltpu.CompilerParams(vmem_limit_bytes=40 * 1024 * 1024),
        name="finish",
    )(gi, ft, fs)
    gin = jnp.transpose(gin, (1, 0, 2)).reshape(latents.shape)
    return gin, gs, gt, gq, go


def solution(mesh):
    in_specs = (
        P("frame", "row", None, None),
        P(),
        P(),
        P(),
        P(),
        P(),
        P("frame", "row", None, None),
    )
    out_specs = (P("frame", "row", None, None), P(), P(), P(), P())
    return jax.shard_map(
        on_device, mesh=mesh, in_specs=in_specs, out_specs=out_specs, check_vma=False
    )
```

```python
import math

import jax
import jax.numpy as jnp
from jax import lax
from jax.experimental import pallas as pl
from jax.experimental.pallas import tpu as pltpu
from jax.sharding import PartitionSpec as P

MESH = pl.DeviceIdType.MESH
BF = jnp.bfloat16
F32 = jnp.float32
HEADS = 8
C = 320
CP = 384
W = 106
WP = 112
ROWS = 2 * WP
UNIT = 128
NR = (768, 960)
GL = 1024
NX, NY, NZ = 4, 4, 8


def nn(a, b):
    return lax.dot_general(a, b, (((1,), (0,)), ((), ())), preferred_element_type=F32)


def nt(a, b):
    return lax.dot_general(a, b, (((1,), (1,)), ((), ())), preferred_element_type=F32)


def tn(a, b):
    return lax.dot_general(a, b, (((0,), (0,)), ((), ())), preferred_element_type=F32)


def widen(x):
    return jnp.concatenate([x, jnp.zeros((x.shape[0], CP - C), x.dtype)], axis=1)


def pack3(a, b, c):
    b = pltpu.roll(b, 64, 1)
    return jnp.concatenate([a[:, :256], a[:, 256:] + b[:, :128], b[:, 128:], c], axis=1)


def silu_grad(v):
    sig = jax.nn.sigmoid(v)
    return sig * (1.0 + v * (1.0 - sig))


def up8(x):
    return jnp.concatenate([x[8:], jnp.zeros((8, x.shape[1]), x.dtype)], axis=0)


def down8(x):
    return jnp.concatenate([jnp.zeros((8, x.shape[1]), x.dtype), x[:-8]], axis=0)


NEAR_LAST = {4: (2, 1, 3), 8: (4, 3, 5, 2, 6, 1, 7)}


def pack2(v):
    r = v.shape[0] // 2
    t = widen(v)[:, 256:]
    return jnp.concatenate([v[:r, :256], v[r:, :256], t[:r] + pltpu.roll(t[r:], 64, 1)], axis=1)


def unpack2(v):
    t = v[:, 512:].astype(F32)
    lo = jnp.concatenate([v[:, :256], t.astype(BF)[:, :64]], axis=1)
    hi = jnp.concatenate([v[:, 256:512], pltpu.roll(t, 64, 1).astype(BF)[:, :64]], axis=1)
    return jnp.concatenate([lo, hi], axis=0)


OUT_BLOCKS = (
    [(640, 256 * j + 128 * r, 128 * r, 128 * j, 128) for j in range(3) for r in range(2)]
    + [(640, 768, 256, 0, 64), (704, 768, 256, 128, 64), (640, 896, 256, 256, 64)]
)


def unpack(x):
    return x[:, :C], pltpu.roll(x[:, 256:640], CP - 64, 1)[:, :C], x[:, 640 : 640 + C]


def mega(
    factor,
    seg_h, lat, cot, wsp_h, wt_h, wqkv_h, wout_h,
    gi, out_t, out_q, out_o, f_s,
    seg, wsp, wt, wqkv, wq, wtr, wout, wo,
    latn, latp, act, hbuf, dhb, zbuf, snd_s, snd_c, rcv_s, rcv_c,
    u_act, u_dt, u_nrm, u_dq, u_mix, u_cot, snd_d, rcv_d,
    dp, dbuf, g_t, g_s, r0, r1, r2, r3, p1, p2, p3, g3, f_t,
    wsem, hs, hr, a_s, a_r, dhs, dhr, s0s, s0r, s1s, s1r, s2s, s2r, s3s, s3r,
):
    fr, row = lax.axis_index("frame"), lax.axis_index("row")
    y, core = fr // 2, fr % 2
    z, x = row // NX, row % NX
    nrow = NX * NZ

    def at(yy, cc, zz, xx):
        return {"frame": yy * 2 + cc, "row": zz * NX + xx}

    def frame_peer(k):
        return {"frame": lax.rem(fr + k, 8), "row": row}

    def row_peer(k):
        return {"frame": fr, "row": lax.rem(row + k + nrow, nrow)}

    i1 = jnp.where(core == 0, x, y)
    i2 = jnp.where(core == 0, y, x)

    def first_peer(k):
        j = lax.rem(i1 + k, 4)
        return j, at(jnp.where(core == 0, y, j), core, z, jnp.where(core == 0, j, x))

    def second_peer(k):
        j = lax.rem(i2 + k, 4)
        return j, at(jnp.where(core == 0, j, y), core, z, jnp.where(core == 0, x, j))

    def z_peer(k):
        j = lax.rem(z + k, NZ)
        return j, at(y, core, j, x)

    sibling = at(y, 1 - core, z, x)

    barrier = pltpu.get_barrier_semaphore()
    peers = [z_peer(k)[1] for k in NEAR_LAST[NZ]]
    peers += [frame_peer(k) for k in NEAR_LAST[8]]
    peers += [row_peer(1), row_peer(-1)]
    peers += [at(y, core, z, lax.rem(x + k, NX)) for k in range(1, NX)]
    for peer in peers:
        pl.semaphore_signal(barrier, inc=1, device_id=peer, device_id_type=MESH)

    loads = [
        pltpu.make_async_copy(s, d, wsem.at[i])
        for i, (s, d) in enumerate(
            [(lat, latn.at[0]), (cot, latn.at[1]), (wqkv_h, wqkv), (wout_h, wout), (wsp_h, wsp), (wt_h, wt), (seg_h, seg)]
        )
    ]
    for cp in loads:
        cp.start()

    def send(src, dst, ssem, rsem, peer):
        cp = pltpu.make_async_remote_copy(
            src_ref=src, dst_ref=dst, send_sem=ssem, recv_sem=rsem,
            device_id=peer, device_id_type=MESH,
        )
        cp.start()
        return cp

    latp[...] = jnp.zeros_like(latp)
    dp[...] = jnp.zeros_like(dp)

    def rows_of(i, dst):
        loads[i].wait()
        v = latn[i].astype(F32)
        for f in range(2):
            dst[f * WP : f * WP + W, :] = v[:, f, :]

    rows_of(0, latp)
    lv = latp[...]
    lv = lv * jax.nn.sigmoid(lv)
    act[1] = lv.astype(BF)
    hbuf[1] = pack2(lv).astype(BF)

    def to_pixels(src, dst):
        halves = [
            jnp.concatenate(
                [src[WP * f + 16 * j + 8 * h : WP * f + 16 * j + 8 * h + 8, :] for j in range(7) for f in range(2)]
                + [jnp.zeros((16, C), F32)],
                axis=0,
            )
            for h in range(2)
        ]
        dst[...] = pack2(jnp.concatenate(halves, axis=0)).astype(BF).reshape(8, 16, 2 * C)

    pl.semaphore_wait(barrier, len(peers))

    halo = [
        send(hbuf.at[1], hbuf.at[0], hs.at[0], hr.at[0], row_peer(1)),
        send(hbuf.at[1], hbuf.at[2], hs.at[1], hr.at[1], row_peer(-1)),
    ]

    def exchange(snd, rcv, ssem, rsem, base):
        cps = []
        for k in NEAR_LAST[8]:
            cps.append(
                send(snd.at[lax.rem(fr + k, 8)], rcv.at[fr],
                     ssem.at[base + k - 1], rsem.at[base + k - 1], frame_peer(k))
            )
        rcv[pl.ds(fr, 1)] = snd[pl.ds(fr, 1)]
        return cps

    rows_of(1, dp)
    to_pixels(dp, snd_c)
    cot_cps = exchange(snd_c, rcv_c, a_s, a_r, 0)

    loads[4].wait()
    for b in range(3):
        zbuf[b] = nn(act[1], wsp[1, b])
    for cp in halo:
        cp.wait_recv()

    def edges(ref):
        @pl.when(row == 0)
        def _():
            ref[0] = jnp.zeros((WP, 2 * C), BF)

        @pl.when(row == nrow - 1)
        def _():
            ref[2] = jnp.zeros((WP, 2 * C), BF)

    edges(hbuf)
    act[0] = unpack2(hbuf[0])
    act[2] = unpack2(hbuf[2])

    for b in range(3):
        zbuf[b] += nn(act[0], wsp[0, b]) + nn(act[2], wsp[2, b])
    rid = lax.broadcasted_iota(jnp.int32, (ROWS, C), 0)
    real = jnp.where(rid >= WP, rid - WP, rid) < W
    sp = latp[...] + pltpu.roll(zbuf[0], 1, 0) + zbuf[1] + pltpu.roll(zbuf[2], ROWS - 1, 0)
    zbuf[0] = jnp.where(real, sp, 0.0)
    to_pixels(zbuf.at[0], snd_s)
    sp_cps = exchange(snd_s, rcv_s, a_s, a_r, 7)

    for i in (2, 3, 5, 6):
        loads[i].wait()
    wo[...] = jnp.zeros_like(wo)
    wo[:C, :] = wout[...]
    for i in range(3):
        if i == 1:
            t = pltpu.roll(wqkv[:, 256:640].astype(F32), CP - 64, 1).astype(BF)
        else:
            t = wqkv[:, 640 * (i // 2) : 640 * (i // 2) + C]
        t = widen(t[:, :C])
        wq[i] = t
        if i > 0:
            wtr[i - 1] = t.T

    ri = lax.broadcasted_iota(jnp.int32, (UNIT, UNIT), 0)
    ci = lax.broadcasted_iota(jnp.int32, (UNIT, UNIT), 1)
    rseg = jnp.zeros((UNIT, UNIT), jnp.int32)
    cseg = jnp.zeros((UNIT, UNIT), jnp.int32)
    nxt = jnp.zeros((UNIT, UNIT), F32)
    prv = jnp.zeros((UNIT, UNIT), F32)
    for f in range(16):
        rseg = jnp.where(ri // 8 == f, seg[f], rseg)
        cseg = jnp.where(ci // 8 == f, seg[f], cseg)
        if f < 15:
            ok = jnp.where(seg[f] == seg[f + 1], 1.0, 0.0).astype(F32)
            nxt = jnp.where(ri // 8 == f, ok, nxt)
            prv = jnp.where(ri // 8 == f + 1, ok, prv)
    bias = jnp.where((rseg == cseg) & (ri % 8 == ci % 8), 0.0, -1e30)

    def wide(m):
        m = jnp.concatenate([m, m, m], axis=1)[:, :C]
        return jnp.concatenate([m, m], axis=0)

    nxt, prv = wide(nxt), wide(prv)
    scale = 1.0 / math.sqrt(C // HEADS)

    for cp in cot_cps:
        cp.wait_recv()
    for cp in sp_cps:
        cp.wait_recv()

    spf = unpack2(rcv_s[...].reshape(UNIT, 2 * C)).astype(F32)
    cotb = unpack2(rcv_c[...].reshape(UNIT, 2 * C))
    am = (spf * jax.nn.sigmoid(spf)).astype(BF)
    u_act[...] = am
    u_cot[...] = cotb
    tmp = spf + nn(am, wt[1])
    tmp = tmp + down8(nn(am, wt[0])) * prv
    tmp = tmp + up8(nn(am, wt[2])) * nxt
    tf = tmp.astype(BF).astype(F32)
    cen = tf - jnp.mean(tf, axis=-1, keepdims=True)
    inv = lax.rsqrt(jnp.mean(cen * cen, axis=-1, keepdims=True) + 1e-05)
    nhat = cen * inv
    nrm = nhat.astype(BF)
    u_nrm[...] = nrm
    qall = nn(nrm, wq[0]).astype(BF)
    kall = nn(nrm, wq[1]).astype(BF)
    vall = nn(nrm, wq[2]).astype(BF)
    kt = nt(wtr[0], nrm)
    vt = nt(wtr[1], nrm)
    dmall = nt(cotb, wo[...]).astype(BF)

    def attention(u):
        rows = slice(UNIT * u, UNIT * u + UNIT)
        state, mixt, dqt = [], [], []
        dk, dv = [None] * 3, [None] * 3
        for hd in range(HEADS):
            lo, hi = 40 * hd, 40 * hd + 40
            t0, t1 = lo // 128, -(-hi // 128)
            w0, w1 = 128 * t0, 128 * t1
            lane = lax.broadcasted_iota(jnp.int32, (UNIT, w1 - w0), 1) + w0
            sel = (lane >= lo) & (lane < hi)
            qm = jnp.where(sel, qall[rows, w0:w1].astype(F32), 0.0).astype(BF)
            dmm = jnp.where(sel, dmall[rows, w0:w1].astype(F32), 0.0).astype(BF)
            state.append((lo, hi, t0, t1, qm, dmm, nt(kall[rows, w0:w1], qm), nt(vall[rows, w0:w1], dmm)))
        second = []
        for lo, hi, t0, t1, qm, dmm, s, dpr in state:
            s = s * scale + bias
            e = jnp.exp(s - jnp.max(s, axis=0, keepdims=True))
            p = e * (1.0 / jnp.sum(e, axis=0, keepdims=True))
            ds = (p * (dpr - jnp.sum(p * dpr, axis=0, keepdims=True)) * scale).astype(BF)
            second.append((lo, hi, t0, t1, qm, dmm, p.astype(BF), ds))
        for lo, hi, t0, t1, qm, dmm, pb, ds in second:
            mixt.append(nn(vt[lo:hi, rows].astype(BF), pb))
            dqt.append(nn(kt[lo:hi, rows].astype(BF), ds))
            for acc, val in ((dk, nn(ds, qm)), (dv, nn(pb, dmm))):
                for t in range(t0, t1):
                    part = val[:, 128 * (t - t0) : 128 * (t - t0) + 128]
                    acc[t] = part if acc[t] is None else acc[t] + part
        u_mix[:, rows] = jnp.concatenate(mixt, axis=0).astype(BF)
        dq = widen(jnp.concatenate(dqt, axis=0).T)
        u_dq[rows, :] = pack3(dq, jnp.concatenate(dk, axis=1), jnp.concatenate(dv, axis=1)).astype(BF)

    attention(0)
    attention(1)
    dn = nt(u_dq[:, : 3 * C], wqkv[...])
    ln = inv * (
        dn
        - jnp.mean(dn, axis=-1, keepdims=True)
        - nhat * jnp.mean(dn * nhat, axis=-1, keepdims=True)
    )
    dt = (cotb.astype(F32) + ln).astype(BF)
    dtf = dt.astype(F32)
    carried = nt(dt, wt[1]) + up8(nt(dt, wt[0])) * nxt + down8(nt(dt, wt[2])) * prv
    snd_d[...] = pack2(dtf + silu_grad(spf) * carried).astype(BF).reshape(8, 16, 2 * C)
    d_cps = exchange(snd_d, rcv_d, a_s, a_r, 14)

    u_dt[...] = pack3(widen(up8(dtf) * nxt), widen(dtf), widen(down8(dtf) * prv)).astype(BF)
    g_t[0:C, :] = tn(u_act[...], u_dt[...]).astype(BF)
    g_t[C : 2 * C, :] = tn(u_nrm[...], u_dq[...]).astype(BF)
    go = widen(nn(u_mix[...], u_cot[...])).astype(BF)
    g_t[2 * C : 2 * C + 128, 768:] = jnp.zeros((128, 256), BF)
    for dst, lane, src, col, n in OUT_BLOCKS:
        g_t[dst : dst + n, lane : lane + 128] = go[src : src + n, col : col + 128]

    bufs = (g_t, g_s)
    outs = (f_t, f_s)
    half = [n // 2 for n in NR]
    quar = [n // 4 for n in NR]
    mine = [pl.multiple_of(core * n, 16) for n in half]
    other = [pl.multiple_of((1 - core) * n, 16) for n in half]
    low = [pl.multiple_of(i2 // 2 * n, 16) for n in quar]
    lane1 = pl.multiple_of(i1 * 256, 256)
    lane2 = pl.multiple_of(i2 % 2 * 128, 128)

    third = [n // 3 for n in half]

    def r0_start(b, c):
        rows = third[b]
        return [
            send(bufs[b].at[pl.ds(pl.multiple_of(other[b] + c * rows, 16), rows), pl.ds(512 * j, 512)],
                 r0.at[b, pl.ds(c * rows, rows), pl.ds(512 * j, 512)],
                 s0s.at[b, 2 * c + j], s0r.at[b, 2 * c + j], sibling)
            for j in range(2)
        ]

    def r0_finish(b, c, cps):
        for cp in cps:
            cp.wait_recv()
        rows = third[b]
        m = pl.ds(pl.multiple_of(mine[b] + c * rows, 16), rows)
        sl = slice(c * rows, c * rows + rows)
        p1[b, sl] = (bufs[b][m, :].astype(F32) + r0[b, sl].astype(F32)).astype(BF)

    def r1_start(b):
        cps = []
        for k in NEAR_LAST[4]:
            j, peer = first_peer(k)
            cps.append(
                send(p1.at[b, pl.ds(0, half[b]), pl.ds(pl.multiple_of(j * 256, 256), 256)],
                     r1.at[b, k - 1, pl.ds(0, half[b])], s1s.at[b, k - 1], s1r.at[b, k - 1], peer)
            )
        return cps

    def r1_finish(b, cps):
        for cp in cps:
            cp.wait_recv()
        t = p1[b, : half[b], pl.ds(lane1, 256)].astype(F32)
        for k in range(3):
            t = t + r1[b, k, : half[b]].astype(F32)
        p2[b, : half[b]] = t.astype(BF)

    def r2_start(b):
        cps = []
        for k in NEAR_LAST[4]:
            j, peer = second_peer(k)
            cps.append(
                send(p2.at[b, pl.ds(pl.multiple_of(j // 2 * quar[b], 16), quar[b]),
                           pl.ds(pl.multiple_of(j % 2 * 128, 128), 128)],
                     r2.at[b, k - 1, pl.ds(0, quar[b])], s2s.at[b, k - 1], s2r.at[b, k - 1], peer)
            )
        return cps

    def r2_finish(b, cps):
        for cp in cps:
            cp.wait_recv()
        t = p2[b, pl.ds(low[b], quar[b]), pl.ds(lane2, 128)].astype(F32)
        for k in range(3):
            t = t + r2[b, k, : quar[b]].astype(F32)
        p3[b, : quar[b]] = t.astype(BF)
        p3[b, quar[b] :] = jnp.zeros((256 - quar[b], 128), BF)

    def r3_start(b):
        cps = []
        for k in NEAR_LAST[NZ]:
            j, peer = z_peer(k)
            cps.append(
                send(p3.at[b, pl.ds(pl.multiple_of(j * 32, 32), 32)], r3.at[b, k - 1],
                     s3s.at[b, k - 1], s3r.at[b, k - 1], peer)
            )
        return cps

    zrow = pl.multiple_of(z * 32, 32)

    def r3_finish(b, cps):
        for cp in cps:
            cp.wait_recv()
        t = p3[b, pl.ds(zrow, 32)].astype(F32)
        for k in range(NZ - 1):
            t = t + r3[b, k].astype(F32)
        g3[b, pl.ds(zrow, 32)] = t.astype(BF)

    def g3_start(b):
        piece = g3.at[b, pl.ds(zrow, 32)]
        return [
            send(piece, piece, s3s.at[b + 2, k - 1], s3r.at[b + 2, k - 1], z_peer(k)[1])
            for k in NEAR_LAST[NZ]
        ]

    def g3_finish(b, cps):
        for cp in cps:
            cp.wait_recv()
        outs[b][pl.ds(pl.multiple_of(mine[b] + low[b], 16), quar[b]),
                pl.ds(pl.multiple_of(lane1 + lane2, 128), 128)] = g3[b, : quar[b]]

    def g2_start(b):
        piece = outs[b].at[pl.ds(pl.multiple_of(mine[b] + low[b], 16), quar[b]),
                           pl.ds(pl.multiple_of(lane1 + lane2, 128), 128)]
        return [
            send(piece, piece, s2s.at[b + 2, k - 1], s2r.at[b + 2, k - 1], second_peer(k)[1])
            for k in NEAR_LAST[4]
        ]

    def block(b, j):
        return outs[b].at[pl.ds(mine[b], half[b]), pl.ds(pl.multiple_of(j * 256, 256), 256)]

    def g1_start(b):
        piece = block(b, i1)
        return [
            send(piece, piece, s1s.at[b + 2, k - 1], s1r.at[b + 2, k - 1], first_peer(k)[1])
            for k in NEAR_LAST[4]
        ]

    def g0_start(b, k):
        lanes = pl.ds(pl.multiple_of(lax.rem(i1 - k + 4, 4) * 256, 256), 256)
        cps = []
        for c in range(3):
            rows = pl.ds(pl.multiple_of(mine[b] + c * third[b], 16), third[b])
            piece = outs[b].at[rows, lanes]
            cps.append(send(piece, piece, s0s.at[b + 2, 3 * k + c], s0r.at[b + 2, 3 * k + c], sibling))
        return cps

    def got(cps):
        for cp in cps:
            cp.wait_recv()

    sent = []

    def keep(cps):
        sent.extend(cps)
        return cps

    t0c = [keep(r0_start(0, c)) for c in range(3)]
    for c in range(3):
        r0_finish(0, c, t0c[c])
    t1c = keep(r1_start(0))

    got(d_cps)
    t = unpack2(rcv_d[...].reshape(UNIT, 2 * C)).astype(F32)
    dv = jnp.concatenate(
        [
            t[UNIT * h + 16 * j + 8 * f : UNIT * h + 16 * j + 8 * f + 8]
            for f in range(2) for j in range(7) for h in range(2)
        ],
        axis=0,
    )
    dp[...] = dv
    dbuf[1] = dv.astype(BF)
    dhb[1] = pack2(dv).astype(BF)
    dcat = pack3(
        widen(pltpu.roll(dv, ROWS - 1, 0)), widen(dv), widen(pltpu.roll(dv, 1, 0))
    ).astype(BF)
    s0c = []
    for a in range(3):
        t = tn(act[a], dcat).astype(BF)
        for c in range(2):
            g_s[c * half[1] + a * 160 : c * half[1] + a * 160 + 160, :] = t[160 * c : 160 * c + 160]
        s0c.append(keep(r0_start(1, a)))
    for a in range(3):
        r0_finish(1, a, s0c[a])
    s1c = keep(r1_start(1))
    r1_finish(0, t1c)
    t2c = keep(r2_start(0))
    r2_finish(0, t2c)
    t3c = keep(r3_start(0))
    r1_finish(1, s1c)
    s2c = keep(r2_start(1))
    dhalo = [
        send(dhb.at[1], dhb.at[0], dhs.at[0], dhr.at[0], row_peer(1)),
        send(dhb.at[1], dhb.at[2], dhs.at[1], dhr.at[1], row_peer(-1)),
    ]
    r3_finish(0, t3c)
    t4c = keep(g3_start(0))
    r2_finish(1, s2c)
    s3c = keep(r3_start(1))
    g3_finish(0, t4c)
    t5c = keep(g2_start(0))

    got(dhalo)

    edges(dhb)
    dbuf[0] = unpack2(dhb[0])
    dbuf[2] = unpack2(dhb[2])

    for b in range(3):
        zbuf[b] = nt(dbuf[2], wsp[0, b]) + nt(dbuf[1], wsp[1, b]) + nt(dbuf[0], wsp[2, b])
    da = pltpu.roll(zbuf[0], ROWS - 1, 0) + zbuf[1] + pltpu.roll(zbuf[2], 1, 0)
    t = dp[...] + silu_grad(latp[...]) * da
    gi[...] = jnp.stack([t[:W], t[WP : WP + W]], axis=1).astype(BF)

    r3_finish(1, s3c)
    s4c = keep(g3_start(1))
    got(t5c)
    t6c = keep(g1_start(0))
    g3_finish(1, s4c)
    s5c = keep(g2_start(1))
    got(s5c)
    s6c = keep(g1_start(1))
    s7c = g0_start(1, 0)
    t7c = g0_start(0, 0)
    for cp, k in zip(t6c, NEAR_LAST[4]):
        cp.wait_recv()
        t7c += g0_start(0, k)
    got(t7c)
    for b, t in enumerate(unpack(f_t[0:C, :].astype(F32) * factor)):
        out_t[b] = t
    out_q[...] = (f_t[C : 2 * C, :].astype(F32) * factor)[:, : 3 * C]
    for dst, lane, src, col, n in OUT_BLOCKS:
        w = min(128, C - col)
        out_o[src : src + n, col : col + w] = f_t[dst : dst + n, lane : lane + w].astype(F32) * factor
    for cp, k in zip(s6c, NEAR_LAST[4]):
        cp.wait_recv()
        s7c += g0_start(1, k)
    keep(t7c + s7c)
    got(s7c)
    for cp in halo + cot_cps + sp_cps + d_cps + dhalo + sent:
        cp.wait_send()


def finish(factor, gi, vt, vq, vo, fs, gin, gs, gt, gq, go, vs, sem):
    cps = []

    def out(src, dst):
        cp = pltpu.make_async_copy(src, dst, sem.at[len(cps)])
        cp.start()
        cps.append(cp)

    for b in range(3):
        out(vt.at[b], gt.at[b])
    for i in range(4):
        r = slice(80 * i, 80 * i + 80)
        out(vq.at[r], gq.at[r])
    out(vo, go)
    out(gi, gin)
    for a in range(3):
        for c in range(2):
            r = c * (NR[1] // 2) + 160 * a
            for b, t in enumerate(unpack(fs[r : r + 160, :].astype(F32) * factor)):
                vs[a, b, 160 * c : 160 * c + 160, :] = t
        for b in range(3):
            out(vs.at[a, b], gs.at[a, b])
    for cp in cps:
        cp.wait()


def on_device(latents, segments, w_spatial, w_temporal, w_qkv, w_out, cotangent):
    vm = pl.BlockSpec(memory_space=pltpu.VMEM)
    anyspec = pl.BlockSpec(memory_space=pl.ANY)
    dma = pltpu.SemaphoreType.DMA
    V = pltpu.VMEM
    hm, qm = max(NR) // 2, max(NR) // 4

    def by_column(t):
        return jnp.transpose(t.reshape(2, W, C), (1, 0, 2))

    factor = 1.0 / math.sqrt(54272)
    shapes = [(3, 3, C, C), (3, C, C), (C, 3 * C), (C, C)]
    inner = pl.pallas_call(
        lambda *refs: mega(factor, *refs),
        out_shape=(jax.ShapeDtypeStruct((W, 2, C), BF),)
        + tuple(jax.ShapeDtypeStruct(s, F32) for s in shapes[1:])
        + (jax.ShapeDtypeStruct((NR[1], GL), BF),),
        in_specs=[pl.BlockSpec(memory_space=pltpu.HBM)] * 7,
        out_specs=(vm,) * 5,
        scratch_shapes=[
            pltpu.SMEM((16,), jnp.int32), V((3, 3, C, C), BF), V((3, C, C), BF), V((C, 3 * C), BF), V((3, C, CP), BF),
            V((2, CP, C), BF), V((C, C), BF), V((CP, C), BF),
            V((2, W, 2, C), BF), V((ROWS, C), F32), V((3, ROWS, C), BF),
            V((3, WP, 2 * C), BF), V((3, WP, 2 * C), BF), V((3, ROWS, C), F32),
            V((8, 16, 2 * C), BF), V((8, 16, 2 * C), BF), V((8, 16, 2 * C), BF), V((8, 16, 2 * C), BF),
            V((2 * UNIT, C), BF), V((2 * UNIT, GL), BF), V((2 * UNIT, C), BF), V((2 * UNIT, GL), BF),
            V((C, 2 * UNIT), BF), V((2 * UNIT, C), BF),
            V((8, 16, 2 * C), BF), V((8, 16, 2 * C), BF),
            V((ROWS, C), F32), V((3, ROWS, C), BF),
            V((NR[0], GL), BF), V((NR[1], GL), BF),
            V((2, hm, GL), BF), V((2, 3, hm, 256), BF), V((2, 3, qm, 128), BF),
            V((2, NZ - 1, 32, 128), BF),
            V((2, hm, GL), BF), V((2, hm, 256), BF), V((2, 256, 128), BF), V((2, 256, 128), BF),
            V((NR[0], GL), BF),
            dma((7,)), dma((2,)), dma((2,)), dma((21,)), dma((21,)), dma((2,)), dma((2,)),
            dma((4, 12)), dma((4, 12)), dma((4, 3)), dma((4, 3)), dma((4, 3)), dma((4, 3)),
            dma((4, NZ - 1)), dma((4, NZ - 1)),
        ],
        compiler_params=pltpu.CompilerParams(
            collective_id=0, has_side_effects=True, vmem_limit_bytes=40 * 1024 * 1024
        ),
        name="mega",
    )(*(
        pltpu.with_memory_space_constraint(t, pltpu.HBM)
        for t in (segments, by_column(latents), by_column(cotangent), w_spatial, w_temporal, w_qkv, w_out)
    ))
    gin, gs, gt, gq, go = pl.pallas_call(
        lambda *refs: finish(factor, *refs),
        out_shape=(jax.ShapeDtypeStruct((W, 2, C), BF),)
        + tuple(jax.ShapeDtypeStruct(s, F32) for s in shapes),
        in_specs=[vm] * 5,
        out_specs=(anyspec,) * 5,
        scratch_shapes=[V(shapes[0], F32), dma((18,))],
        compiler_params=pltpu.CompilerParams(vmem_limit_bytes=40 * 1024 * 1024),
        name="finish",
    )(*inner)
    gin = jnp.transpose(gin, (1, 0, 2)).reshape(latents.shape)
    return gin, gs, gt, gq, go


def solution(mesh):
    in_specs = (
        P("frame", "row", None, None),
        P(),
        P(),
        P(),
        P(),
        P(),
        P("frame", "row", None, None),
    )
    out_specs = (P("frame", "row", None, None), P(), P(), P(), P())
    return jax.shard_map(
        on_device, mesh=mesh, in_specs=in_specs, out_specs=out_specs, check_vma=False
    )
```

```python
import math

import jax
import jax.numpy as jnp
from jax import lax
from jax.experimental import pallas as pl
from jax.experimental.pallas import tpu as pltpu
from jax.sharding import PartitionSpec as P

MESH = pl.DeviceIdType.MESH
BF = jnp.bfloat16
F32 = jnp.float32
HEADS = 8
C = 320
CP = 384
W = 106
WP = 112
ROWS = 2 * WP
UNIT = 128
NR = (768, 960)
GL = 1024
NX, NY, NZ = 4, 4, 8


def nn(a, b):
    return lax.dot_general(a, b, (((1,), (0,)), ((), ())), preferred_element_type=F32)


def nt(a, b):
    return lax.dot_general(a, b, (((1,), (1,)), ((), ())), preferred_element_type=F32)


def tn(a, b):
    return lax.dot_general(a, b, (((0,), (0,)), ((), ())), preferred_element_type=F32)


def widen(x):
    return jnp.concatenate([x, jnp.zeros((x.shape[0], CP - C), x.dtype)], axis=1)


def pack3(a, b, c):
    b = pltpu.roll(b, 64, 1)
    return jnp.concatenate([a[:, :256], a[:, 256:] + b[:, :128], b[:, 128:], c], axis=1)


def silu_grad(v):
    sig = jax.nn.sigmoid(v)
    return sig * (1.0 + v * (1.0 - sig))


def up8(x):
    return jnp.concatenate([x[8:], jnp.zeros((8, x.shape[1]), x.dtype)], axis=0)


def down8(x):
    return jnp.concatenate([jnp.zeros((8, x.shape[1]), x.dtype), x[:-8]], axis=0)


NEAR_LAST = {4: (2, 1, 3), 8: (4, 3, 5, 2, 6, 1, 7)}


def pack2(v):
    r = v.shape[0] // 2
    t = widen(v)[:, 256:]
    return jnp.concatenate([v[:r, :256], v[r:, :256], t[:r] + pltpu.roll(t[r:], 64, 1)], axis=1)


def unpack2(v):
    t = v[:, 512:].astype(F32)
    lo = jnp.concatenate([v[:, :256], t.astype(BF)[:, :64]], axis=1)
    hi = jnp.concatenate([v[:, 256:512], pltpu.roll(t, 64, 1).astype(BF)[:, :64]], axis=1)
    return jnp.concatenate([lo, hi], axis=0)


MAIN = 384
REST = 96

OUT_BLOCKS = (
    [(640, 256 * j + 128 * r, 128 * r, 128 * j, 128) for j in range(3) for r in range(2)]
    + [(640, 768, 256, 0, 64), (704, 768, 256, 128, 64), (640, 896, 256, 256, 64)]
)


def unpack(x):
    return x[:, :C], pltpu.roll(x[:, 256:640], CP - 64, 1)[:, :C], x[:, 640 : 640 + C]


def mega(
    factor,
    seg_h, lat, cot, wsp_h, wt_h, wqkv_h, wout_h,
    gi, out_t, out_q, out_o, f_s,
    seg, wsp, wt, wqkv, wq, wtr, wout, wo,
    latn, latp, act, hbuf, dhb, zbuf, snd_s, snd_c, rcv_s, rcv_c,
    u_act, u_dt, u_nrm, u_dq, u_mix, u_cot, snd_d, rcv_d,
    dp, dbuf, g_t, g_s, r0, r1, r2, r3, p1, p2, p3, g3, f_t, zr, zx, zy,
    wsem, hs, hr, a_s, a_r, dhs, dhr, s0s, s0r, s1s, s1r, s2s, s2r, s3s, s3r, zs, zv,
):
    fr, row = lax.axis_index("frame"), lax.axis_index("row")
    y, core = fr // 2, fr % 2
    z, x = row // NX, row % NX
    nrow = NX * NZ

    def at(yy, cc, zz, xx):
        return {"frame": yy * 2 + cc, "row": zz * NX + xx}

    def frame_peer(k):
        return {"frame": lax.rem(fr + k, 8), "row": row}

    def row_peer(k):
        return {"frame": fr, "row": lax.rem(row + k + nrow, nrow)}

    i1 = jnp.where(core == 0, x, y)
    i2 = jnp.where(core == 0, y, x)

    def first_peer(k):
        j = lax.rem(i1 + k, 4)
        return j, at(jnp.where(core == 0, y, j), core, z, jnp.where(core == 0, j, x))

    def second_peer(k):
        j = lax.rem(i2 + k, 4)
        return j, at(jnp.where(core == 0, j, y), core, z, jnp.where(core == 0, x, j))

    def z_peer(k):
        j = lax.rem(z + k, NZ)
        return j, at(y, core, j, x)

    sibling = at(y, 1 - core, z, x)

    barrier = pltpu.get_barrier_semaphore()
    peers = [z_peer(k)[1] for k in NEAR_LAST[NZ]]
    peers += [frame_peer(k) for k in NEAR_LAST[8]]
    peers += [row_peer(1), row_peer(-1)]
    peers += [at(y, core, z, lax.rem(x + k, NX)) for k in range(1, NX)]
    for peer in peers:
        pl.semaphore_signal(barrier, inc=1, device_id=peer, device_id_type=MESH)

    loads = [
        pltpu.make_async_copy(s, d, wsem.at[i])
        for i, (s, d) in enumerate(
            [(lat, latn.at[0]), (cot, latn.at[1]), (wqkv_h, wqkv), (wout_h, wout), (wsp_h, wsp), (wt_h, wt), (seg_h, seg)]
        )
    ]
    for cp in loads:
        cp.start()

    def send(src, dst, ssem, rsem, peer):
        cp = pltpu.make_async_remote_copy(
            src_ref=src, dst_ref=dst, send_sem=ssem, recv_sem=rsem,
            device_id=peer, device_id_type=MESH,
        )
        cp.start()
        return cp

    latp[...] = jnp.zeros_like(latp)
    dp[...] = jnp.zeros_like(dp)

    def rows_of(i, dst):
        loads[i].wait()
        v = latn[i].astype(F32)
        for f in range(2):
            dst[f * WP : f * WP + W, :] = v[:, f, :]

    rows_of(0, latp)
    lv = latp[...]
    lv = lv * jax.nn.sigmoid(lv)
    act[1] = lv.astype(BF)
    hbuf[1] = pack2(lv).astype(BF)

    def to_pixels(src, dst):
        halves = [
            jnp.concatenate(
                [src[WP * f + 16 * j + 8 * h : WP * f + 16 * j + 8 * h + 8, :] for j in range(7) for f in range(2)]
                + [jnp.zeros((16, C), F32)],
                axis=0,
            )
            for h in range(2)
        ]
        dst[...] = pack2(jnp.concatenate(halves, axis=0)).astype(BF).reshape(8, 16, 2 * C)

    pl.semaphore_wait(barrier, len(peers))

    halo = [
        send(hbuf.at[1], hbuf.at[0], hs.at[0], hr.at[0], row_peer(1)),
        send(hbuf.at[1], hbuf.at[2], hs.at[1], hr.at[1], row_peer(-1)),
    ]

    def exchange(snd, rcv, ssem, rsem, base):
        cps = []
        for k in NEAR_LAST[8]:
            cps.append(
                send(snd.at[lax.rem(fr + k, 8)], rcv.at[fr],
                     ssem.at[base + k - 1], rsem.at[base + k - 1], frame_peer(k))
            )
        rcv[pl.ds(fr, 1)] = snd[pl.ds(fr, 1)]
        return cps

    rows_of(1, dp)
    to_pixels(dp, snd_c)
    cot_cps = exchange(snd_c, rcv_c, a_s, a_r, 0)

    loads[4].wait()
    for b in range(3):
        zbuf[b] = nn(act[1], wsp[1, b])
    for cp in halo:
        cp.wait_recv()

    def edges(ref):
        @pl.when(row == 0)
        def _():
            ref[0] = jnp.zeros((WP, 2 * C), BF)

        @pl.when(row == nrow - 1)
        def _():
            ref[2] = jnp.zeros((WP, 2 * C), BF)

    edges(hbuf)
    act[0] = unpack2(hbuf[0])
    act[2] = unpack2(hbuf[2])

    for b in range(3):
        zbuf[b] += nn(act[0], wsp[0, b]) + nn(act[2], wsp[2, b])
    rid = lax.broadcasted_iota(jnp.int32, (ROWS, C), 0)
    real = jnp.where(rid >= WP, rid - WP, rid) < W
    sp = latp[...] + pltpu.roll(zbuf[0], 1, 0) + zbuf[1] + pltpu.roll(zbuf[2], ROWS - 1, 0)
    zbuf[0] = jnp.where(real, sp, 0.0)
    to_pixels(zbuf.at[0], snd_s)
    sp_cps = exchange(snd_s, rcv_s, a_s, a_r, 7)

    for i in (2, 3, 5, 6):
        loads[i].wait()
    wo[...] = jnp.zeros_like(wo)
    wo[:C, :] = wout[...]
    for i in range(3):
        if i == 1:
            t = pltpu.roll(wqkv[:, 256:640].astype(F32), CP - 64, 1).astype(BF)
        else:
            t = wqkv[:, 640 * (i // 2) : 640 * (i // 2) + C]
        t = widen(t[:, :C])
        wq[i] = t
        if i > 0:
            wtr[i - 1] = t.T

    ri = lax.broadcasted_iota(jnp.int32, (UNIT, UNIT), 0)
    ci = lax.broadcasted_iota(jnp.int32, (UNIT, UNIT), 1)
    rseg = jnp.zeros((UNIT, UNIT), jnp.int32)
    cseg = jnp.zeros((UNIT, UNIT), jnp.int32)
    nxt = jnp.zeros((UNIT, UNIT), F32)
    prv = jnp.zeros((UNIT, UNIT), F32)
    for f in range(16):
        rseg = jnp.where(ri // 8 == f, seg[f], rseg)
        cseg = jnp.where(ci // 8 == f, seg[f], cseg)
        if f < 15:
            ok = jnp.where(seg[f] == seg[f + 1], 1.0, 0.0).astype(F32)
            nxt = jnp.where(ri // 8 == f, ok, nxt)
            prv = jnp.where(ri // 8 == f + 1, ok, prv)
    bias = jnp.where((rseg == cseg) & (ri % 8 == ci % 8), 0.0, -1e30)

    def wide(m):
        m = jnp.concatenate([m, m, m], axis=1)[:, :C]
        return jnp.concatenate([m, m], axis=0)

    nxt, prv = wide(nxt), wide(prv)
    scale = 1.0 / math.sqrt(C // HEADS)

    for cp in cot_cps:
        cp.wait_recv()
    for cp in sp_cps:
        cp.wait_recv()

    spf = unpack2(rcv_s[...].reshape(UNIT, 2 * C)).astype(F32)
    cotb = unpack2(rcv_c[...].reshape(UNIT, 2 * C))
    am = (spf * jax.nn.sigmoid(spf)).astype(BF)
    u_act[...] = am
    u_cot[...] = cotb
    tmp = spf + nn(am, wt[1])
    tmp = tmp + down8(nn(am, wt[0])) * prv
    tmp = tmp + up8(nn(am, wt[2])) * nxt
    tf = tmp.astype(BF).astype(F32)
    cen = tf - jnp.mean(tf, axis=-1, keepdims=True)
    inv = lax.rsqrt(jnp.mean(cen * cen, axis=-1, keepdims=True) + 1e-05)
    nhat = cen * inv
    nrm = nhat.astype(BF)
    u_nrm[...] = nrm
    qall = nn(nrm, wq[0]).astype(BF)
    kall = nn(nrm, wq[1]).astype(BF)
    vall = nn(nrm, wq[2]).astype(BF)
    kt = nt(wtr[0], nrm)
    vt = nt(wtr[1], nrm)
    dmall = nt(cotb, wo[...]).astype(BF)

    def attention(u):
        rows = slice(UNIT * u, UNIT * u + UNIT)
        state, mixt, dqt = [], [], []
        dk, dv = [None] * 3, [None] * 3
        for hd in range(HEADS):
            lo, hi = 40 * hd, 40 * hd + 40
            t0, t1 = lo // 128, -(-hi // 128)
            w0, w1 = 128 * t0, 128 * t1
            lane = lax.broadcasted_iota(jnp.int32, (UNIT, w1 - w0), 1) + w0
            sel = (lane >= lo) & (lane < hi)
            qm = jnp.where(sel, qall[rows, w0:w1].astype(F32), 0.0).astype(BF)
            dmm = jnp.where(sel, dmall[rows, w0:w1].astype(F32), 0.0).astype(BF)
            state.append((lo, hi, t0, t1, qm, dmm, nt(kall[rows, w0:w1], qm), nt(vall[rows, w0:w1], dmm)))
        second = []
        for lo, hi, t0, t1, qm, dmm, s, dpr in state:
            s = s * scale + bias
            e = jnp.exp(s - jnp.max(s, axis=0, keepdims=True))
            p = e * (1.0 / jnp.sum(e, axis=0, keepdims=True))
            ds = (p * (dpr - jnp.sum(p * dpr, axis=0, keepdims=True)) * scale).astype(BF)
            second.append((lo, hi, t0, t1, qm, dmm, p.astype(BF), ds))
        for lo, hi, t0, t1, qm, dmm, pb, ds in second:
            mixt.append(nn(vt[lo:hi, rows].astype(BF), pb))
            dqt.append(nn(kt[lo:hi, rows].astype(BF), ds))
            for acc, val in ((dk, nn(ds, qm)), (dv, nn(pb, dmm))):
                for t in range(t0, t1):
                    part = val[:, 128 * (t - t0) : 128 * (t - t0) + 128]
                    acc[t] = part if acc[t] is None else acc[t] + part
        u_mix[:, rows] = jnp.concatenate(mixt, axis=0).astype(BF)
        dq = widen(jnp.concatenate(dqt, axis=0).T)
        u_dq[rows, :] = pack3(dq, jnp.concatenate(dk, axis=1), jnp.concatenate(dv, axis=1)).astype(BF)

    attention(0)
    attention(1)
    dn = nt(u_dq[:, : 3 * C], wqkv[...])
    ln = inv * (
        dn
        - jnp.mean(dn, axis=-1, keepdims=True)
        - nhat * jnp.mean(dn * nhat, axis=-1, keepdims=True)
    )
    dt = (cotb.astype(F32) + ln).astype(BF)
    dtf = dt.astype(F32)
    carried = nt(dt, wt[1]) + up8(nt(dt, wt[0])) * nxt + down8(nt(dt, wt[2])) * prv
    snd_d[...] = pack2(dtf + silu_grad(spf) * carried).astype(BF).reshape(8, 16, 2 * C)
    d_cps = exchange(snd_d, rcv_d, a_s, a_r, 14)

    u_dt[...] = pack3(widen(up8(dtf) * nxt), widen(dtf), widen(down8(dtf) * prv)).astype(BF)
    g_t[0:C, :] = tn(u_act[...], u_dt[...]).astype(BF)
    g_t[C : 2 * C, :] = tn(u_nrm[...], u_dq[...]).astype(BF)
    go = widen(nn(u_mix[...], u_cot[...])).astype(BF)
    g_t[2 * C : 2 * C + 128, 768:] = jnp.zeros((128, 256), BF)
    for dst, lane, src, col, n in OUT_BLOCKS:
        g_t[dst : dst + n, lane : lane + 128] = go[src : src + n, col : col + 128]

    bufs = (g_t, g_s)
    outs = (f_t, f_s)
    half = [n // 2 for n in NR]
    quar = [MAIN // 2] * 2
    mine = [pl.multiple_of(core * n, 16) for n in half]
    other = [pl.multiple_of((1 - core) * n, 16) for n in half]
    low = [pl.multiple_of(i2 // 2 * n, 16) for n in quar]
    lane1 = pl.multiple_of(i1 * 256, 256)
    lane2 = pl.multiple_of(i2 % 2 * 128, 128)

    third = [n // 3 for n in half]

    def r0_start(b, c):
        rows = third[b]
        return [
            send(bufs[b].at[pl.ds(pl.multiple_of(other[b] + c * rows, 16), rows), pl.ds(512 * j, 512)],
                 r0.at[b, pl.ds(c * rows, rows), pl.ds(512 * j, 512)],
                 s0s.at[b, 2 * c + j], s0r.at[b, 2 * c + j], sibling)
            for j in range(2)
        ]

    def r0_finish(b, c, cps):
        for cp in cps:
            cp.wait_recv()
        rows = third[b]
        m = pl.ds(pl.multiple_of(mine[b] + c * rows, 16), rows)
        sl = slice(c * rows, c * rows + rows)
        p1[b, sl] = (bufs[b][m, :].astype(F32) + r0[b, sl].astype(F32)).astype(BF)

    def r1_start(b):
        cps = []
        for k in NEAR_LAST[4]:
            j, peer = first_peer(k)
            cps.append(
                send(p1.at[b, pl.ds(0, MAIN), pl.ds(pl.multiple_of(j * 256, 256), 256)],
                     r1.at[b, k - 1, pl.ds(0, MAIN)], s1s.at[b, k - 1], s1r.at[b, k - 1], peer)
            )
        return cps

    def r1_finish(b, cps):
        for cp in cps:
            cp.wait_recv()
        t = p1[b, : MAIN, pl.ds(lane1, 256)].astype(F32)
        for k in range(3):
            t = t + r1[b, k, : MAIN].astype(F32)
        p2[b, : MAIN] = t.astype(BF)

    def r2_start(b):
        cps = []
        for k in NEAR_LAST[4]:
            j, peer = second_peer(k)
            cps.append(
                send(p2.at[b, pl.ds(pl.multiple_of(j // 2 * quar[b], 16), quar[b]),
                           pl.ds(pl.multiple_of(j % 2 * 128, 128), 128)],
                     r2.at[b, k - 1, pl.ds(0, quar[b])], s2s.at[b, k - 1], s2r.at[b, k - 1], peer)
            )
        return cps

    def r2_finish(b, cps):
        for cp in cps:
            cp.wait_recv()
        t = p2[b, pl.ds(low[b], quar[b]), pl.ds(lane2, 128)].astype(F32)
        for k in range(3):
            t = t + r2[b, k, : quar[b]].astype(F32)
        p3[b, : quar[b]] = t.astype(BF)
        p3[b, quar[b] :] = jnp.zeros((256 - quar[b], 128), BF)

    def r3_start(b):
        cps = []
        for k in NEAR_LAST[NZ]:
            j, peer = z_peer(k)
            cps.append(
                send(p3.at[b, pl.ds(pl.multiple_of(j * 32, 32), 32)], r3.at[b, k - 1],
                     s3s.at[b, k - 1], s3r.at[b, k - 1], peer)
            )
        return cps

    zrow = pl.multiple_of(z * 32, 32)

    def r3_finish(b, cps):
        for cp in cps:
            cp.wait_recv()
        t = p3[b, pl.ds(zrow, 32)].astype(F32)
        for k in range(NZ - 1):
            t = t + r3[b, k].astype(F32)
        g3[b, pl.ds(zrow, 32)] = t.astype(BF)

    def g3_start(b):
        piece = g3.at[b, pl.ds(zrow, 32)]
        return [
            send(piece, piece, s3s.at[b + 2, k - 1], s3r.at[b + 2, k - 1], z_peer(k)[1])
            for k in NEAR_LAST[NZ]
        ]

    def g3_finish(b, cps):
        for cp in cps:
            cp.wait_recv()
        outs[b][pl.ds(pl.multiple_of(mine[b] + low[b], 16), quar[b]),
                pl.ds(pl.multiple_of(lane1 + lane2, 128), 128)] = g3[b, : quar[b]]

    def g2_start(b):
        piece = outs[b].at[pl.ds(pl.multiple_of(mine[b] + low[b], 16), quar[b]),
                           pl.ds(pl.multiple_of(lane1 + lane2, 128), 128)]
        return [
            send(piece, piece, s2s.at[b + 2, k - 1], s2r.at[b + 2, k - 1], second_peer(k)[1])
            for k in NEAR_LAST[4]
        ]

    def block(b, j):
        return outs[b].at[pl.ds(mine[b], MAIN), pl.ds(pl.multiple_of(j * 256, 256), 256)]

    def g1_start(b):
        piece = block(b, i1)
        return [
            send(piece, piece, s1s.at[b + 2, k - 1], s1r.at[b + 2, k - 1], first_peer(k)[1])
            for k in NEAR_LAST[4]
        ]

    def g0_start(b, k):
        lanes = pl.ds(pl.multiple_of(lax.rem(i1 - k + 4, 4) * 256, 256), 256)
        cps = []
        for c in range(3):
            rows = pl.ds(pl.multiple_of(mine[b] + c * (MAIN // 3), 16), MAIN // 3)
            piece = outs[b].at[rows, lanes]
            cps.append(send(piece, piece, s0s.at[b + 2, 3 * k + c], s0r.at[b + 2, 3 * k + c], sibling))
        return cps

    def got(cps):
        for cp in cps:
            cp.wait_recv()

    zlane = pl.multiple_of(z * 128, 128)
    rest = pl.ds(pl.multiple_of(mine[1] + MAIN, 16), REST)

    def z1_start():
        cps = []
        for k in NEAR_LAST[NZ]:
            j, peer = z_peer(k)
            cps.append(
                send(p1.at[1, pl.ds(MAIN, REST), pl.ds(pl.multiple_of(j * 128, 128), 128)],
                     zr.at[k - 1], zs.at[0, k - 1], zv.at[0, k - 1], peer)
            )
        return cps

    def z1_finish(cps):
        got(cps)
        t = p1[1, MAIN : MAIN + REST, pl.ds(zlane, 128)].astype(F32)
        for k in range(NZ - 1):
            t = t + zr[k].astype(F32)
        zx[pl.ds(i1, 1)] = t.astype(BF)[None]

    def spread(ref, place, sem, peer_of):
        piece = ref.at[place]
        return [
            send(piece, piece, zs.at[sem, k - 1], zv.at[sem, k - 1], peer_of(k)[1])
            for k in NEAR_LAST[4]
        ]

    def in_order(ref):
        t = ref[0].astype(F32)
        for k in range(1, 4):
            t = t + ref[k].astype(F32)
        return t.astype(BF)

    def z4_start():
        piece = f_s.at[rest, pl.ds(zlane, 128)]
        return [
            send(piece, piece, zs.at[3, k - 1], zv.at[3, k - 1], z_peer(k)[1])
            for k in NEAR_LAST[NZ]
        ]

    def z0_start():
        cps = []
        for j in range(2):
            piece = f_s.at[rest, pl.ds(512 * j, 512)]
            cps.append(send(piece, piece, s0s.at[3, 12 + j], s0r.at[3, 12 + j], sibling))
        return cps

    sent = []

    def keep(cps):
        sent.extend(cps)
        return cps

    t0c = [keep(r0_start(0, c)) for c in range(3)]
    for c in range(3):
        r0_finish(0, c, t0c[c])
    t1c = keep(r1_start(0))

    got(d_cps)
    t = unpack2(rcv_d[...].reshape(UNIT, 2 * C)).astype(F32)
    dv = jnp.concatenate(
        [
            t[UNIT * h + 16 * j + 8 * f : UNIT * h + 16 * j + 8 * f + 8]
            for f in range(2) for j in range(7) for h in range(2)
        ],
        axis=0,
    )
    dp[...] = dv
    dbuf[1] = dv.astype(BF)
    dhb[1] = pack2(dv).astype(BF)
    dcat = pack3(
        widen(pltpu.roll(dv, ROWS - 1, 0)), widen(dv), widen(pltpu.roll(dv, 1, 0))
    ).astype(BF)
    s0c = []
    for a in range(3):
        t = tn(act[a], dcat).astype(BF)
        for c in range(2):
            g_s[c * half[1] + a * 160 : c * half[1] + a * 160 + 160, :] = t[160 * c : 160 * c + 160]
        s0c.append(keep(r0_start(1, a)))
    for a in range(3):
        r0_finish(1, a, s0c[a])
    s1c = keep(r1_start(1))
    z1c = keep(z1_start())
    r1_finish(0, t1c)
    t2c = keep(r2_start(0))
    r2_finish(0, t2c)
    t3c = keep(r3_start(0))
    r1_finish(1, s1c)
    s2c = keep(r2_start(1))
    dhalo = [
        send(dhb.at[1], dhb.at[0], dhs.at[0], dhr.at[0], row_peer(1)),
        send(dhb.at[1], dhb.at[2], dhs.at[1], dhr.at[1], row_peer(-1)),
    ]
    z1_finish(z1c)
    z2c = keep(spread(zx, i1, 1, first_peer))
    r3_finish(0, t3c)
    t4c = keep(g3_start(0))
    r2_finish(1, s2c)
    s3c = keep(r3_start(1))
    got(z2c)
    zy[pl.ds(i2, 1)] = in_order(zx)[None]
    z3c = keep(spread(zy, i2, 2, second_peer))
    g3_finish(0, t4c)
    t5c = keep(g2_start(0))

    got(dhalo)

    edges(dhb)
    dbuf[0] = unpack2(dhb[0])
    dbuf[2] = unpack2(dhb[2])

    for b in range(3):
        zbuf[b] = nt(dbuf[2], wsp[0, b]) + nt(dbuf[1], wsp[1, b]) + nt(dbuf[0], wsp[2, b])
    da = pltpu.roll(zbuf[0], ROWS - 1, 0) + zbuf[1] + pltpu.roll(zbuf[2], 1, 0)
    t = dp[...] + silu_grad(latp[...]) * da
    gi[...] = jnp.stack([t[:W], t[WP : WP + W]], axis=1).astype(BF)

    r3_finish(1, s3c)
    s4c = keep(g3_start(1))
    got(z3c)
    f_s[rest, pl.ds(zlane, 128)] = in_order(zy)
    got(t5c)
    t6c = keep(g1_start(0))
    g3_finish(1, s4c)
    s5c = keep(g2_start(1))
    z4c = keep(z4_start())
    got(s5c)
    s6c = keep(g1_start(1))
    s7c = g0_start(1, 0)
    t7c = g0_start(0, 0)
    for cp, k in zip(t6c, NEAR_LAST[4]):
        cp.wait_recv()
        t7c += g0_start(0, k)
    got(z4c)
    s7c += z0_start()
    for cp, k in zip(s6c, NEAR_LAST[4]):
        cp.wait_recv()
        s7c += g0_start(1, k)
    got(t7c)
    for b, t in enumerate(unpack(f_t[0:C, :].astype(F32) * factor)):
        out_t[b] = t
    out_q[...] = (f_t[C : 2 * C, :].astype(F32) * factor)[:, : 3 * C]
    for dst, lane, src, col, n in OUT_BLOCKS:
        w = min(128, C - col)
        out_o[src : src + n, col : col + w] = f_t[dst : dst + n, lane : lane + w].astype(F32) * factor
    keep(t7c + s7c)
    got(s7c)
    for cp in halo + cot_cps + sp_cps + d_cps + dhalo + sent:
        cp.wait_send()


def finish(factor, gi, vt, vq, vo, fs, gin, gs, gt, gq, go, vs, sem):
    cps = []

    def out(src, dst):
        cp = pltpu.make_async_copy(src, dst, sem.at[len(cps)])
        cp.start()
        cps.append(cp)

    for b in range(3):
        out(vt.at[b], gt.at[b])
    for i in range(4):
        r = slice(80 * i, 80 * i + 80)
        out(vq.at[r], gq.at[r])
    out(vo, go)
    out(gi, gin)
    for a in range(3):
        for c in range(2):
            r = c * (NR[1] // 2) + 160 * a
            for b, t in enumerate(unpack(fs[r : r + 160, :].astype(F32) * factor)):
                vs[a, b, 160 * c : 160 * c + 160, :] = t
        for b in range(3):
            out(vs.at[a, b], gs.at[a, b])
    for cp in cps:
        cp.wait()


def on_device(latents, segments, w_spatial, w_temporal, w_qkv, w_out, cotangent):
    vm = pl.BlockSpec(memory_space=pltpu.VMEM)
    anyspec = pl.BlockSpec(memory_space=pl.ANY)
    dma = pltpu.SemaphoreType.DMA
    V = pltpu.VMEM
    hm = max(NR) // 2

    def by_column(t):
        return jnp.transpose(t.reshape(2, W, C), (1, 0, 2))

    factor = 1.0 / math.sqrt(54272)
    shapes = [(3, 3, C, C), (3, C, C), (C, 3 * C), (C, C)]
    inner = pl.pallas_call(
        lambda *refs: mega(factor, *refs),
        out_shape=(jax.ShapeDtypeStruct((W, 2, C), BF),)
        + tuple(jax.ShapeDtypeStruct(s, F32) for s in shapes[1:])
        + (jax.ShapeDtypeStruct((NR[1], GL), BF),),
        in_specs=[pl.BlockSpec(memory_space=pltpu.HBM)] * 7,
        out_specs=(vm,) * 5,
        scratch_shapes=[
            pltpu.SMEM((16,), jnp.int32), V((3, 3, C, C), BF), V((3, C, C), BF), V((C, 3 * C), BF), V((3, C, CP), BF),
            V((2, CP, C), BF), V((C, C), BF), V((CP, C), BF),
            V((2, W, 2, C), BF), V((ROWS, C), F32), V((3, ROWS, C), BF),
            V((3, WP, 2 * C), BF), V((3, WP, 2 * C), BF), V((3, ROWS, C), F32),
            V((8, 16, 2 * C), BF), V((8, 16, 2 * C), BF), V((8, 16, 2 * C), BF), V((8, 16, 2 * C), BF),
            V((2 * UNIT, C), BF), V((2 * UNIT, GL), BF), V((2 * UNIT, C), BF), V((2 * UNIT, GL), BF),
            V((C, 2 * UNIT), BF), V((2 * UNIT, C), BF),
            V((8, 16, 2 * C), BF), V((8, 16, 2 * C), BF),
            V((ROWS, C), F32), V((3, ROWS, C), BF),
            V((NR[0], GL), BF), V((NR[1], GL), BF),
            V((2, hm, GL), BF), V((2, 3, MAIN, 256), BF), V((2, 3, MAIN // 2, 128), BF),
            V((2, NZ - 1, 32, 128), BF),
            V((2, hm, GL), BF), V((2, MAIN, 256), BF), V((2, 256, 128), BF), V((2, 256, 128), BF),
            V((NR[0], GL), BF), V((NZ - 1, REST, 128), BF), V((4, REST, 128), BF), V((4, REST, 128), BF),
            dma((7,)), dma((2,)), dma((2,)), dma((21,)), dma((21,)), dma((2,)), dma((2,)),
            dma((4, 14)), dma((4, 14)), dma((4, 3)), dma((4, 3)), dma((4, 3)), dma((4, 3)),
            dma((4, NZ - 1)), dma((4, NZ - 1)), dma((4, NZ - 1)), dma((4, NZ - 1)),
        ],
        compiler_params=pltpu.CompilerParams(
            collective_id=0, has_side_effects=True, vmem_limit_bytes=40 * 1024 * 1024
        ),
        name="mega",
    )(*(
        pltpu.with_memory_space_constraint(t, pltpu.HBM)
        for t in (segments, by_column(latents), by_column(cotangent), w_spatial, w_temporal, w_qkv, w_out)
    ))
    gin, gs, gt, gq, go = pl.pallas_call(
        lambda *refs: finish(factor, *refs),
        out_shape=(jax.ShapeDtypeStruct((W, 2, C), BF),)
        + tuple(jax.ShapeDtypeStruct(s, F32) for s in shapes),
        in_specs=[vm] * 5,
        out_specs=(anyspec,) * 5,
        scratch_shapes=[V(shapes[0], F32), dma((18,))],
        compiler_params=pltpu.CompilerParams(vmem_limit_bytes=40 * 1024 * 1024),
        name="finish",
    )(*inner)
    gin = jnp.transpose(gin, (1, 0, 2)).reshape(latents.shape)
    return gin, gs, gt, gq, go


def solution(mesh):
    in_specs = (
        P("frame", "row", None, None),
        P(),
        P(),
        P(),
        P(),
        P(),
        P("frame", "row", None, None),
    )
    out_specs = (P("frame", "row", None, None), P(), P(), P(), P())
    return jax.shard_map(
        on_device, mesh=mesh, in_specs=in_specs, out_specs=out_specs, check_vma=False
    )
```

```python
import math

import jax
import jax.numpy as jnp
from jax import lax
from jax.experimental import pallas as pl
from jax.experimental.pallas import tpu as pltpu
from jax.sharding import PartitionSpec as P

MESH = pl.DeviceIdType.MESH
BF = jnp.bfloat16
F32 = jnp.float32
HEADS = 8
C = 320
CP = 384
W = 106
WP = 112
ROWS = 2 * WP
UNIT = 128
NR = (768, 960)
GL = 1024
NX, NY, NZ = 4, 4, 8


def nn(a, b):
    return lax.dot_general(a, b, (((1,), (0,)), ((), ())), preferred_element_type=F32)


def nt(a, b):
    return lax.dot_general(a, b, (((1,), (1,)), ((), ())), preferred_element_type=F32)


def tn(a, b):
    return lax.dot_general(a, b, (((0,), (0,)), ((), ())), preferred_element_type=F32)


def widen(x):
    return jnp.concatenate([x, jnp.zeros((x.shape[0], CP - C), x.dtype)], axis=1)


def pack3(a, b, c):
    b = pltpu.roll(b, 64, 1)
    return jnp.concatenate([a[:, :256], a[:, 256:] + b[:, :128], b[:, 128:], c], axis=1)


def silu_grad(v):
    sig = jax.nn.sigmoid(v)
    return sig * (1.0 + v * (1.0 - sig))


def up8(x):
    return jnp.concatenate([x[8:], jnp.zeros((8, x.shape[1]), x.dtype)], axis=0)


def down8(x):
    return jnp.concatenate([jnp.zeros((8, x.shape[1]), x.dtype), x[:-8]], axis=0)


NEAR_LAST = {4: (2, 1, 3), 8: (4, 3, 5, 2, 6, 1, 7)}


def pack2(v):
    r = v.shape[0] // 2
    t = widen(v)[:, 256:]
    return jnp.concatenate([v[:r, :256], v[r:, :256], t[:r] + pltpu.roll(t[r:], 64, 1)], axis=1)


def unpack2(v):
    t = v[:, 512:].astype(F32)
    lo = jnp.concatenate([v[:, :256], t.astype(BF)[:, :64]], axis=1)
    hi = jnp.concatenate([v[:, 256:512], pltpu.roll(t, 64, 1).astype(BF)[:, :64]], axis=1)
    return jnp.concatenate([lo, hi], axis=0)


MAIN = 384
REST = 96

OUT_BLOCKS = (
    [(640, 256 * j + 128 * r, 128 * r, 128 * j, 128) for j in range(3) for r in range(2)]
    + [(640, 768, 256, 0, 64), (704, 768, 256, 128, 64), (640, 896, 256, 256, 64)]
)


def unpack(x):
    return x[:, :C], pltpu.roll(x[:, 256:640], CP - 64, 1)[:, :C], x[:, 640 : 640 + C]


def mega(
    factor,
    seg_h, lat, cot, wsp_h, wt_h, wqkv_h, wout_h,
    gi, out_t, out_q, out_o, f_s,
    seg, wsp, wt, wqkv, wq, wtr, wout, wo,
    latn, latp, act, hbuf, dhb, zbuf, snd_s, snd_c, rcv_s, rcv_c,
    u_act, u_dt, u_nrm, u_dq, u_mix, u_cot, snd_d, rcv_d,
    dp, dbuf, g_t, g_s, r0, r1, r2, r3, p1, p2, p3, g3, f_t, zr, zx, zy,
    wsem, hs, hr, a_s, a_r, dhs, dhr, s0s, s0r, s1s, s1r, s2s, s2r, s3s, s3r, zs, zv,
):
    fr, row = lax.axis_index("frame"), lax.axis_index("row")
    y, core = fr // 2, fr % 2
    z, x = row // NX, row % NX
    nrow = NX * NZ

    def at(yy, cc, zz, xx):
        return {"frame": yy * 2 + cc, "row": zz * NX + xx}

    def frame_peer(k):
        return {"frame": lax.rem(fr + k, 8), "row": row}

    def row_peer(k):
        return {"frame": fr, "row": lax.rem(row + k + nrow, nrow)}

    i1 = jnp.where(core == 0, x, y)
    i2 = jnp.where(core == 0, y, x)

    def first_peer(k):
        j = lax.rem(i1 + k, 4)
        return j, at(jnp.where(core == 0, y, j), core, z, jnp.where(core == 0, j, x))

    def second_peer(k):
        j = lax.rem(i2 + k, 4)
        return j, at(jnp.where(core == 0, j, y), core, z, jnp.where(core == 0, x, j))

    def z_peer(k):
        j = lax.rem(z + k, NZ)
        return j, at(y, core, j, x)

    sibling = at(y, 1 - core, z, x)

    barrier = pltpu.get_barrier_semaphore()
    peers = [z_peer(k)[1] for k in NEAR_LAST[NZ]]
    peers += [frame_peer(k) for k in NEAR_LAST[8]]
    peers += [row_peer(1), row_peer(-1)]
    peers += [at(y, core, z, lax.rem(x + k, NX)) for k in range(1, NX)]
    for peer in peers:
        pl.semaphore_signal(barrier, inc=1, device_id=peer, device_id_type=MESH)

    loads = [
        pltpu.make_async_copy(s, d, wsem.at[i])
        for i, (s, d) in enumerate(
            [(lat, latn.at[0]), (cot, latn.at[1]), (wqkv_h, wqkv), (wout_h, wout), (wsp_h, wsp), (wt_h, wt), (seg_h, seg)]
        )
    ]
    for cp in loads:
        cp.start()

    def send(src, dst, ssem, rsem, peer):
        cp = pltpu.make_async_remote_copy(
            src_ref=src, dst_ref=dst, send_sem=ssem, recv_sem=rsem,
            device_id=peer, device_id_type=MESH,
        )
        cp.start()
        return cp

    latp[...] = jnp.zeros_like(latp)
    dp[...] = jnp.zeros_like(dp)

    def rows_of(i, dst):
        loads[i].wait()
        v = latn[i].astype(F32)
        for f in range(2):
            dst[f * WP : f * WP + W, :] = v[:, f, :]

    rows_of(0, latp)
    lv = latp[...]
    lv = lv * jax.nn.sigmoid(lv)
    act[1] = lv.astype(BF)
    hbuf[1] = pack2(lv).astype(BF)

    def to_pixels(src, dst):
        halves = [
            jnp.concatenate(
                [src[WP * f + 16 * j + 8 * h : WP * f + 16 * j + 8 * h + 8, :] for j in range(7) for f in range(2)]
                + [jnp.zeros((16, C), F32)],
                axis=0,
            )
            for h in range(2)
        ]
        dst[...] = pack2(jnp.concatenate(halves, axis=0)).astype(BF).reshape(8, 16, 2 * C)

    pl.semaphore_wait(barrier, len(peers))

    halo = [
        send(hbuf.at[1], hbuf.at[0], hs.at[0], hr.at[0], row_peer(1)),
        send(hbuf.at[1], hbuf.at[2], hs.at[1], hr.at[1], row_peer(-1)),
    ]

    def exchange(snd, rcv, ssem, rsem, base):
        cps = []
        for k in NEAR_LAST[8]:
            cps.append(
                send(snd.at[lax.rem(fr + k, 8)], rcv.at[fr],
                     ssem.at[base + k - 1], rsem.at[base + k - 1], frame_peer(k))
            )
        rcv[pl.ds(fr, 1)] = snd[pl.ds(fr, 1)]
        return cps

    rows_of(1, dp)
    to_pixels(dp, snd_c)
    cot_cps = exchange(snd_c, rcv_c, a_s, a_r, 0)

    loads[4].wait()
    for b in range(3):
        zbuf[b] = nn(act[1], wsp[1, b])
    for cp in halo:
        cp.wait_recv()

    def edges(ref):
        @pl.when(row == 0)
        def _():
            ref[0] = jnp.zeros((WP, 2 * C), BF)

        @pl.when(row == nrow - 1)
        def _():
            ref[2] = jnp.zeros((WP, 2 * C), BF)

    edges(hbuf)
    act[0] = unpack2(hbuf[0])
    act[2] = unpack2(hbuf[2])

    for b in range(3):
        zbuf[b] += nn(act[0], wsp[0, b]) + nn(act[2], wsp[2, b])
    rid = lax.broadcasted_iota(jnp.int32, (ROWS, C), 0)
    real = jnp.where(rid >= WP, rid - WP, rid) < W
    sp = latp[...] + pltpu.roll(zbuf[0], 1, 0) + zbuf[1] + pltpu.roll(zbuf[2], ROWS - 1, 0)
    zbuf[0] = jnp.where(real, sp, 0.0)
    to_pixels(zbuf.at[0], snd_s)
    sp_cps = exchange(snd_s, rcv_s, a_s, a_r, 7)

    for i in (2, 3, 5, 6):
        loads[i].wait()
    wo[...] = jnp.zeros_like(wo)
    wo[:C, :] = wout[...]
    for i in range(3):
        if i == 1:
            t = pltpu.roll(wqkv[:, 256:640].astype(F32), CP - 64, 1).astype(BF)
        else:
            t = wqkv[:, 640 * (i // 2) : 640 * (i // 2) + C]
        t = widen(t[:, :C])
        wq[i] = t
        if i > 0:
            wtr[i - 1] = t.T

    ri = lax.broadcasted_iota(jnp.int32, (UNIT, UNIT), 0)
    ci = lax.broadcasted_iota(jnp.int32, (UNIT, UNIT), 1)
    rseg = jnp.zeros((UNIT, UNIT), jnp.int32)
    cseg = jnp.zeros((UNIT, UNIT), jnp.int32)
    nxt = jnp.zeros((UNIT, UNIT), F32)
    prv = jnp.zeros((UNIT, UNIT), F32)
    for f in range(16):
        rseg = jnp.where(ri // 8 == f, seg[f], rseg)
        cseg = jnp.where(ci // 8 == f, seg[f], cseg)
        if f < 15:
            ok = jnp.where(seg[f] == seg[f + 1], 1.0, 0.0).astype(F32)
            nxt = jnp.where(ri // 8 == f, ok, nxt)
            prv = jnp.where(ri // 8 == f + 1, ok, prv)
    bias = jnp.where((rseg == cseg) & (ri % 8 == ci % 8), 0.0, -1e30)

    def wide(m):
        m = jnp.concatenate([m, m, m], axis=1)[:, :C]
        return jnp.concatenate([m, m], axis=0)

    nxt, prv = wide(nxt), wide(prv)
    scale = 1.0 / math.sqrt(C // HEADS)

    for cp in cot_cps:
        cp.wait_recv()
    for cp in sp_cps:
        cp.wait_recv()

    spf = unpack2(rcv_s[...].reshape(UNIT, 2 * C)).astype(F32)
    cotb = unpack2(rcv_c[...].reshape(UNIT, 2 * C))
    am = (spf * jax.nn.sigmoid(spf)).astype(BF)
    u_act[...] = am
    u_cot[...] = cotb
    tmp = spf + nn(am, wt[1])
    tmp = tmp + down8(nn(am, wt[0])) * prv
    tmp = tmp + up8(nn(am, wt[2])) * nxt
    tf = tmp.astype(BF).astype(F32)
    cen = tf - jnp.mean(tf, axis=-1, keepdims=True)
    inv = lax.rsqrt(jnp.mean(cen * cen, axis=-1, keepdims=True) + 1e-05)
    nhat = cen * inv
    nrm = nhat.astype(BF)
    u_nrm[...] = nrm
    qall = nn(nrm, wq[0]).astype(BF)
    kall = nn(nrm, wq[1]).astype(BF)
    vall = nn(nrm, wq[2]).astype(BF)
    kt = nt(wtr[0], nrm)
    vt = nt(wtr[1], nrm)
    dmall = nt(cotb, wo[...]).astype(BF)

    def attention(u):
        rows = slice(UNIT * u, UNIT * u + UNIT)
        state, mixt, dqt = [], [], []
        dk, dv = [None] * 3, [None] * 3
        for hd in range(HEADS):
            lo, hi = 40 * hd, 40 * hd + 40
            t0, t1 = lo // 128, -(-hi // 128)
            w0, w1 = 128 * t0, 128 * t1
            lane = lax.broadcasted_iota(jnp.int32, (UNIT, w1 - w0), 1) + w0
            sel = (lane >= lo) & (lane < hi)
            qm = jnp.where(sel, qall[rows, w0:w1].astype(F32), 0.0).astype(BF)
            dmm = jnp.where(sel, dmall[rows, w0:w1].astype(F32), 0.0).astype(BF)
            state.append((lo, hi, t0, t1, qm, dmm, nt(kall[rows, w0:w1], qm), nt(vall[rows, w0:w1], dmm)))
        second = []
        for lo, hi, t0, t1, qm, dmm, s, dpr in state:
            s = s * scale + bias
            e = jnp.exp(s - jnp.max(s, axis=0, keepdims=True))
            p = e * (1.0 / jnp.sum(e, axis=0, keepdims=True))
            ds = (p * (dpr - jnp.sum(p * dpr, axis=0, keepdims=True)) * scale).astype(BF)
            second.append((lo, hi, t0, t1, qm, dmm, p.astype(BF), ds))
        for lo, hi, t0, t1, qm, dmm, pb, ds in second:
            mixt.append(nn(vt[lo:hi, rows].astype(BF), pb))
            dqt.append(nn(kt[lo:hi, rows].astype(BF), ds))
            for acc, val in ((dk, nn(ds, qm)), (dv, nn(pb, dmm))):
                for t in range(t0, t1):
                    part = val[:, 128 * (t - t0) : 128 * (t - t0) + 128]
                    acc[t] = part if acc[t] is None else acc[t] + part
        u_mix[:, rows] = jnp.concatenate(mixt, axis=0).astype(BF)
        dq = widen(jnp.concatenate(dqt, axis=0).T)
        u_dq[rows, :] = pack3(dq, jnp.concatenate(dk, axis=1), jnp.concatenate(dv, axis=1)).astype(BF)

    attention(0)
    attention(1)
    dn = nt(u_dq[:, : 3 * C], wqkv[...])
    ln = inv * (
        dn
        - jnp.mean(dn, axis=-1, keepdims=True)
        - nhat * jnp.mean(dn * nhat, axis=-1, keepdims=True)
    )
    dt = (cotb.astype(F32) + ln).astype(BF)
    dtf = dt.astype(F32)
    carried = nt(dt, wt[1]) + up8(nt(dt, wt[0])) * nxt + down8(nt(dt, wt[2])) * prv
    snd_d[...] = pack2(dtf + silu_grad(spf) * carried).astype(BF).reshape(8, 16, 2 * C)
    d_cps = exchange(snd_d, rcv_d, a_s, a_r, 14)

    u_dt[...] = pack3(widen(up8(dtf) * nxt), widen(dtf), widen(down8(dtf) * prv)).astype(BF)
    g_t[0:C, :] = tn(u_act[...], u_dt[...]).astype(BF)
    g_t[C : 2 * C, :] = tn(u_nrm[...], u_dq[...]).astype(BF)
    go = widen(nn(u_mix[...], u_cot[...])).astype(BF)
    g_t[2 * C : 2 * C + 128, 768:] = jnp.zeros((128, 256), BF)
    for dst, lane, src, col, n in OUT_BLOCKS:
        g_t[dst : dst + n, lane : lane + 128] = go[src : src + n, col : col + 128]

    bufs = (g_t, g_s)
    outs = (f_t, f_s)
    half = [n // 2 for n in NR]
    quar = [MAIN // 2] * 2
    mine = [pl.multiple_of(core * n, 16) for n in half]
    other = [pl.multiple_of((1 - core) * n, 16) for n in half]
    low = [pl.multiple_of(i2 // 2 * n, 16) for n in quar]
    lane1 = pl.multiple_of(i1 * 256, 256)
    lane2 = pl.multiple_of(i2 % 2 * 128, 128)

    third = [n // 3 for n in half]

    def r0_start(b, c):
        rows = third[b]
        return [
            send(bufs[b].at[pl.ds(pl.multiple_of(other[b] + c * rows, 16), rows), pl.ds(512 * j, 512)],
                 r0.at[b, pl.ds(c * rows, rows), pl.ds(512 * j, 512)],
                 s0s.at[b, 2 * c + j], s0r.at[b, 2 * c + j], sibling)
            for j in range(2)
        ]

    def r0_finish(b, c, cps):
        for cp in cps:
            cp.wait_recv()
        rows = third[b]
        m = pl.ds(pl.multiple_of(mine[b] + c * rows, 16), rows)
        sl = slice(c * rows, c * rows + rows)
        p1[b, sl] = (bufs[b][m, :].astype(F32) + r0[b, sl].astype(F32)).astype(BF)

    def r1_start(b):
        cps = []
        for k in NEAR_LAST[4]:
            j, peer = first_peer(k)
            cps.append(
                send(p1.at[b, pl.ds(0, MAIN), pl.ds(pl.multiple_of(j * 256, 256), 256)],
                     r1.at[b, k - 1, pl.ds(0, MAIN)], s1s.at[b, k - 1], s1r.at[b, k - 1], peer)
            )
        return cps

    def r1_finish(b, cps):
        for cp in cps:
            cp.wait_recv()
        t = p1[b, : MAIN, pl.ds(lane1, 256)].astype(F32)
        for k in range(3):
            t = t + r1[b, k, : MAIN].astype(F32)
        p2[b, : MAIN] = t.astype(BF)

    def r2_start(b):
        cps = []
        for k in NEAR_LAST[4]:
            j, peer = second_peer(k)
            cps.append(
                send(p2.at[b, pl.ds(pl.multiple_of(j // 2 * quar[b], 16), quar[b]),
                           pl.ds(pl.multiple_of(j % 2 * 128, 128), 128)],
                     r2.at[b, k - 1, pl.ds(0, quar[b])], s2s.at[b, k - 1], s2r.at[b, k - 1], peer)
            )
        return cps

    def r2_finish(b, cps):
        for cp in cps:
            cp.wait_recv()
        t = p2[b, pl.ds(low[b], quar[b]), pl.ds(lane2, 128)].astype(F32)
        for k in range(3):
            t = t + r2[b, k, : quar[b]].astype(F32)
        p3[b, : quar[b]] = t.astype(BF)
        p3[b, quar[b] :] = jnp.zeros((256 - quar[b], 128), BF)

    def r3_start(b):
        cps = []
        for k in NEAR_LAST[NZ]:
            j, peer = z_peer(k)
            cps.append(
                send(p3.at[b, pl.ds(pl.multiple_of(j * 32, 32), 32)], r3.at[b, k - 1],
                     s3s.at[b, k - 1], s3r.at[b, k - 1], peer)
            )
        return cps

    zrow = pl.multiple_of(z * 32, 32)

    def r3_finish(b, cps):
        for cp in cps:
            cp.wait_recv()
        t = p3[b, pl.ds(zrow, 32)].astype(F32)
        for k in range(NZ - 1):
            t = t + r3[b, k].astype(F32)
        g3[b, pl.ds(zrow, 32)] = t.astype(BF)

    def g3_start(b):
        piece = g3.at[b, pl.ds(zrow, 32)]
        return [
            send(piece, piece, s3s.at[b + 2, k - 1], s3r.at[b + 2, k - 1], z_peer(k)[1])
            for k in NEAR_LAST[NZ]
        ]

    def g3_finish(b, cps):
        for cp in cps:
            cp.wait_recv()
        outs[b][pl.ds(pl.multiple_of(mine[b] + low[b], 16), quar[b]),
                pl.ds(pl.multiple_of(lane1 + lane2, 128), 128)] = g3[b, : quar[b]]

    def g2_start(b):
        piece = outs[b].at[pl.ds(pl.multiple_of(mine[b] + low[b], 16), quar[b]),
                           pl.ds(pl.multiple_of(lane1 + lane2, 128), 128)]
        return [
            send(piece, piece, s2s.at[b + 2, k - 1], s2r.at[b + 2, k - 1], second_peer(k)[1])
            for k in NEAR_LAST[4]
        ]

    def block(b, j):
        return outs[b].at[pl.ds(mine[b], MAIN), pl.ds(pl.multiple_of(j * 256, 256), 256)]

    def g1_start(b):
        piece = block(b, i1)
        return [
            send(piece, piece, s1s.at[b + 2, k - 1], s1r.at[b + 2, k - 1], first_peer(k)[1])
            for k in NEAR_LAST[4]
        ]

    def g0_start(b, k):
        lanes = pl.ds(pl.multiple_of(lax.rem(i1 - k + 4, 4) * 256, 256), 256)
        cps = []
        for c in range(3):
            rows = pl.ds(pl.multiple_of(mine[b] + c * (MAIN // 3), 16), MAIN // 3)
            piece = outs[b].at[rows, lanes]
            cps.append(send(piece, piece, s0s.at[b + 2, 3 * k + c], s0r.at[b + 2, 3 * k + c], sibling))
        return cps

    def got(cps):
        for cp in cps:
            cp.wait_recv()

    zlane = pl.multiple_of(z * 128, 128)
    rest = pl.ds(pl.multiple_of(mine[1] + MAIN, 16), REST)

    def z1_start():
        cps = []
        for k in NEAR_LAST[NZ]:
            j, peer = z_peer(k)
            cps.append(
                send(p1.at[1, pl.ds(MAIN, REST), pl.ds(pl.multiple_of(j * 128, 128), 128)],
                     zr.at[k - 1], zs.at[0, k - 1], zv.at[0, k - 1], peer)
            )
        return cps

    def z1_finish(cps):
        got(cps)
        t = p1[1, MAIN : MAIN + REST, pl.ds(zlane, 128)].astype(F32)
        for k in range(NZ - 1):
            t = t + zr[k].astype(F32)
        zx[pl.ds(i1, 1)] = t.astype(BF)[None]

    def spread(ref, place, sem, peer_of):
        piece = ref.at[place]
        return [
            send(piece, piece, zs.at[sem, k - 1], zv.at[sem, k - 1], peer_of(k)[1])
            for k in NEAR_LAST[4]
        ]

    def in_order(ref):
        t = ref[0].astype(F32)
        for k in range(1, 4):
            t = t + ref[k].astype(F32)
        return t.astype(BF)

    def z4_start():
        piece = f_s.at[rest, pl.ds(zlane, 128)]
        return [
            send(piece, piece, zs.at[3, k - 1], zv.at[3, k - 1], z_peer(k)[1])
            for k in NEAR_LAST[NZ]
        ]

    def z0_start():
        cps = []
        for j in range(2):
            piece = f_s.at[rest, pl.ds(512 * j, 512)]
            cps.append(send(piece, piece, s0s.at[3, 12 + j], s0r.at[3, 12 + j], sibling))
        return cps

    sent = []

    def keep(cps):
        sent.extend(cps)
        return cps

    t0c = [keep(r0_start(0, c)) for c in range(3)]
    for c in range(3):
        r0_finish(0, c, t0c[c])
    t1c = keep(r1_start(0))

    got(d_cps)
    t = unpack2(rcv_d[...].reshape(UNIT, 2 * C)).astype(F32)
    dv = jnp.concatenate(
        [
            t[UNIT * h + 16 * j + 8 * f : UNIT * h + 16 * j + 8 * f + 8]
            for f in range(2) for j in range(7) for h in range(2)
        ],
        axis=0,
    )
    dp[...] = dv
    dbuf[1] = dv.astype(BF)
    dcat = pack3(
        widen(pltpu.roll(dv, ROWS - 1, 0)), widen(dv), widen(pltpu.roll(dv, 1, 0))
    ).astype(BF)
    s0c = []
    for a in range(3):
        t = tn(act[a], dcat).astype(BF)
        for c in range(2):
            g_s[c * half[1] + a * 160 : c * half[1] + a * 160 + 160, :] = t[160 * c : 160 * c + 160]
        s0c.append(keep(r0_start(1, a)))
    for a in range(3):
        r0_finish(1, a, s0c[a])
    s1c = keep(r1_start(1))
    z1c = keep(z1_start())
    r1_finish(0, t1c)
    t2c = keep(r2_start(0))
    r2_finish(0, t2c)
    t3c = keep(r3_start(0))
    r1_finish(1, s1c)
    s2c = keep(r2_start(1))
    dhb[1] = pack2(dv).astype(BF)
    dhalo = [
        send(dhb.at[1], dhb.at[0], dhs.at[0], dhr.at[0], row_peer(1)),
        send(dhb.at[1], dhb.at[2], dhs.at[1], dhr.at[1], row_peer(-1)),
    ]
    z1_finish(z1c)
    z2c = keep(spread(zx, i1, 1, first_peer))
    r3_finish(0, t3c)
    t4c = keep(g3_start(0))
    r2_finish(1, s2c)
    s3c = keep(r3_start(1))
    g3_finish(0, t4c)
    t5c = keep(g2_start(0))
    got(z2c)
    zy[pl.ds(i2, 1)] = in_order(zx)[None]
    z3c = keep(spread(zy, i2, 2, second_peer))

    got(dhalo)

    edges(dhb)
    dbuf[0] = unpack2(dhb[0])
    dbuf[2] = unpack2(dhb[2])

    for b in range(3):
        zbuf[b] = nt(dbuf[2], wsp[0, b]) + nt(dbuf[1], wsp[1, b]) + nt(dbuf[0], wsp[2, b])
    da = pltpu.roll(zbuf[0], ROWS - 1, 0) + zbuf[1] + pltpu.roll(zbuf[2], 1, 0)
    t = dp[...] + silu_grad(latp[...]) * da
    gi[...] = jnp.stack([t[:W], t[WP : WP + W]], axis=1).astype(BF)

    r3_finish(1, s3c)
    s4c = keep(g3_start(1))
    got(t5c)
    t6c = keep(g1_start(0))
    got(z3c)
    f_s[rest, pl.ds(zlane, 128)] = in_order(zy)
    g3_finish(1, s4c)
    s5c = keep(g2_start(1))
    z4c = keep(z4_start())
    got(s5c)
    s6c = keep(g1_start(1))
    s7c = g0_start(1, 0)
    t7c = g0_start(0, 0)
    for cp, k in zip(t6c, NEAR_LAST[4]):
        cp.wait_recv()
        t7c += g0_start(0, k)
    got(z4c)
    s7c += z0_start()
    for cp, k in zip(s6c, NEAR_LAST[4]):
        cp.wait_recv()
        s7c += g0_start(1, k)
    got(t7c)
    for b, t in enumerate(unpack(f_t[0:C, :].astype(F32) * factor)):
        out_t[b] = t
    out_q[...] = (f_t[C : 2 * C, :].astype(F32) * factor)[:, : 3 * C]
    for dst, lane, src, col, n in OUT_BLOCKS:
        w = min(128, C - col)
        out_o[src : src + n, col : col + w] = f_t[dst : dst + n, lane : lane + w].astype(F32) * factor
    keep(t7c + s7c)
    got(s7c)
    for cp in halo + cot_cps + sp_cps + d_cps + dhalo + sent:
        cp.wait_send()


def finish(factor, gi, vt, vq, vo, fs, gin, gs, gt, gq, go, vs, sem):
    cps = []

    def out(src, dst):
        cp = pltpu.make_async_copy(src, dst, sem.at[len(cps)])
        cp.start()
        cps.append(cp)

    for b in range(3):
        out(vt.at[b], gt.at[b])
    for i in range(4):
        r = slice(80 * i, 80 * i + 80)
        out(vq.at[r], gq.at[r])
    out(vo, go)
    out(gi, gin)
    for a in range(3):
        for c in range(2):
            r = c * (NR[1] // 2) + 160 * a
            for b, t in enumerate(unpack(fs[r : r + 160, :].astype(F32) * factor)):
                vs[a, b, 160 * c : 160 * c + 160, :] = t
        for b in range(3):
            out(vs.at[a, b], gs.at[a, b])
    for cp in cps:
        cp.wait()


def on_device(latents, segments, w_spatial, w_temporal, w_qkv, w_out, cotangent):
    vm = pl.BlockSpec(memory_space=pltpu.VMEM)
    anyspec = pl.BlockSpec(memory_space=pl.ANY)
    dma = pltpu.SemaphoreType.DMA
    V = pltpu.VMEM
    hm = max(NR) // 2

    def by_column(t):
        return jnp.transpose(t.reshape(2, W, C), (1, 0, 2))

    factor = 1.0 / math.sqrt(54272)
    shapes = [(3, 3, C, C), (3, C, C), (C, 3 * C), (C, C)]
    inner = pl.pallas_call(
        lambda *refs: mega(factor, *refs),
        out_shape=(jax.ShapeDtypeStruct((W, 2, C), BF),)
        + tuple(jax.ShapeDtypeStruct(s, F32) for s in shapes[1:])
        + (jax.ShapeDtypeStruct((NR[1], GL), BF),),
        in_specs=[pl.BlockSpec(memory_space=pltpu.HBM)] * 7,
        out_specs=(vm,) * 5,
        scratch_shapes=[
            pltpu.SMEM((16,), jnp.int32), V((3, 3, C, C), BF), V((3, C, C), BF), V((C, 3 * C), BF), V((3, C, CP), BF),
            V((2, CP, C), BF), V((C, C), BF), V((CP, C), BF),
            V((2, W, 2, C), BF), V((ROWS, C), F32), V((3, ROWS, C), BF),
            V((3, WP, 2 * C), BF), V((3, WP, 2 * C), BF), V((3, ROWS, C), F32),
            V((8, 16, 2 * C), BF), V((8, 16, 2 * C), BF), V((8, 16, 2 * C), BF), V((8, 16, 2 * C), BF),
            V((2 * UNIT, C), BF), V((2 * UNIT, GL), BF), V((2 * UNIT, C), BF), V((2 * UNIT, GL), BF),
            V((C, 2 * UNIT), BF), V((2 * UNIT, C), BF),
            V((8, 16, 2 * C), BF), V((8, 16, 2 * C), BF),
            V((ROWS, C), F32), V((3, ROWS, C), BF),
            V((NR[0], GL), BF), V((NR[1], GL), BF),
            V((2, hm, GL), BF), V((2, 3, MAIN, 256), BF), V((2, 3, MAIN // 2, 128), BF),
            V((2, NZ - 1, 32, 128), BF),
            V((2, hm, GL), BF), V((2, MAIN, 256), BF), V((2, 256, 128), BF), V((2, 256, 128), BF),
            V((NR[0], GL), BF), V((NZ - 1, REST, 128), BF), V((4, REST, 128), BF), V((4, REST, 128), BF),
            dma((7,)), dma((2,)), dma((2,)), dma((21,)), dma((21,)), dma((2,)), dma((2,)),
            dma((4, 14)), dma((4, 14)), dma((4, 3)), dma((4, 3)), dma((4, 3)), dma((4, 3)),
            dma((4, NZ - 1)), dma((4, NZ - 1)), dma((4, NZ - 1)), dma((4, NZ - 1)),
        ],
        compiler_params=pltpu.CompilerParams(
            collective_id=0, has_side_effects=True, vmem_limit_bytes=40 * 1024 * 1024
        ),
        name="mega",
    )(*(
        pltpu.with_memory_space_constraint(t, pltpu.HBM)
        for t in (segments, by_column(latents), by_column(cotangent), w_spatial, w_temporal, w_qkv, w_out)
    ))
    gin, gs, gt, gq, go = pl.pallas_call(
        lambda *refs: finish(factor, *refs),
        out_shape=(jax.ShapeDtypeStruct((W, 2, C), BF),)
        + tuple(jax.ShapeDtypeStruct(s, F32) for s in shapes),
        in_specs=[vm] * 5,
        out_specs=(anyspec,) * 5,
        scratch_shapes=[V(shapes[0], F32), dma((18,))],
        compiler_params=pltpu.CompilerParams(vmem_limit_bytes=40 * 1024 * 1024),
        name="finish",
    )(*inner)
    gin = jnp.transpose(gin, (1, 0, 2)).reshape(latents.shape)
    return gin, gs, gt, gq, go


def solution(mesh):
    in_specs = (
        P("frame", "row", None, None),
        P(),
        P(),
        P(),
        P(),
        P(),
        P("frame", "row", None, None),
    )
    out_specs = (P("frame", "row", None, None), P(), P(), P(), P())
    return jax.shard_map(
        on_device, mesh=mesh, in_specs=in_specs, out_specs=out_specs, check_vma=False
    )
```

```python
import math

import jax
import jax.numpy as jnp
from jax import lax
from jax.experimental import pallas as pl
from jax.experimental.pallas import tpu as pltpu
from jax.sharding import PartitionSpec as P

MESH = pl.DeviceIdType.MESH
BF = jnp.bfloat16
F32 = jnp.float32
HEADS = 8
C = 320
CP = 384
W = 106
WP = 112
ROWS = 2 * WP
UNIT = 128
NR = (768, 960)
GL = 1024
NX, NY, NZ = 4, 4, 8


def nn(a, b):
    return lax.dot_general(a, b, (((1,), (0,)), ((), ())), preferred_element_type=F32)


def nt(a, b):
    return lax.dot_general(a, b, (((1,), (1,)), ((), ())), preferred_element_type=F32)


def tn(a, b):
    return lax.dot_general(a, b, (((0,), (0,)), ((), ())), preferred_element_type=F32)


def widen(x):
    return jnp.concatenate([x, jnp.zeros((x.shape[0], CP - C), x.dtype)], axis=1)


def pack3(a, b, c):
    b = pltpu.roll(b, 64, 1)
    return jnp.concatenate([a[:, :256], a[:, 256:] + b[:, :128], b[:, 128:], c], axis=1)


def silu_grad(v):
    sig = jax.nn.sigmoid(v)
    return sig * (1.0 + v * (1.0 - sig))


def up8(x):
    return jnp.concatenate([x[8:], jnp.zeros((8, x.shape[1]), x.dtype)], axis=0)


def down8(x):
    return jnp.concatenate([jnp.zeros((8, x.shape[1]), x.dtype), x[:-8]], axis=0)


NEAR_LAST = {4: (2, 1, 3), 8: (4, 3, 5, 2, 6, 1, 7)}


def pack2(v):
    r = v.shape[0] // 2
    t = widen(v)[:, 256:]
    return jnp.concatenate([v[:r, :256], v[r:, :256], t[:r] + pltpu.roll(t[r:], 64, 1)], axis=1)


def unpack2(v):
    t = v[:, 512:].astype(F32)
    lo = jnp.concatenate([v[:, :256], t.astype(BF)[:, :64]], axis=1)
    hi = jnp.concatenate([v[:, 256:512], pltpu.roll(t, 64, 1).astype(BF)[:, :64]], axis=1)
    return jnp.concatenate([lo, hi], axis=0)


MAIN = 384
REST = 96

OUT_BLOCKS = (
    [(640, 256 * j + 128 * r, 128 * r, 128 * j, 128) for j in range(3) for r in range(2)]
    + [(640, 768, 256, 0, 64), (704, 768, 256, 128, 64), (640, 896, 256, 256, 64)]
)


def unpack(x):
    return x[:, :C], pltpu.roll(x[:, 256:640], CP - 64, 1)[:, :C], x[:, 640 : 640 + C]


def mega(
    factor,
    seg_h, lat, cot, wsp_h, wt_h, wqkv_h, wout_h,
    gi, out_t, out_q, out_o, f_s,
    seg, wsp, wt, wqkv, wq, wtr, wout, wo,
    latn, latp, act, hbuf, dhb, zbuf, snd_s, snd_c, rcv_s, rcv_c,
    u_act, u_dt, u_nrm, u_dq, u_mix, u_cot, snd_d, rcv_d,
    dp, dbuf, g_t, g_s, r0, r1, r2, r3, p1, p2, p3, g3, f_t, zr, zx, zy,
    wsem, hs, hr, a_s, a_r, dhs, dhr, s0s, s0r, s1s, s1r, s2s, s2r, s3s, s3r, zs, zv,
):
    fr, row = lax.axis_index("frame"), lax.axis_index("row")
    y, core = fr // 2, fr % 2
    z, x = row // NX, row % NX
    nrow = NX * NZ

    def at(yy, cc, zz, xx):
        return {"frame": yy * 2 + cc, "row": zz * NX + xx}

    def frame_peer(k):
        return {"frame": lax.rem(fr + k, 8), "row": row}

    def row_peer(k):
        return {"frame": fr, "row": lax.rem(row + k + nrow, nrow)}

    i1 = jnp.where(core == 0, x, y)
    i2 = jnp.where(core == 0, y, x)

    def first_peer(k):
        j = lax.rem(i1 + k, 4)
        return j, at(jnp.where(core == 0, y, j), core, z, jnp.where(core == 0, j, x))

    def second_peer(k):
        j = lax.rem(i2 + k, 4)
        return j, at(jnp.where(core == 0, j, y), core, z, jnp.where(core == 0, x, j))

    def z_peer(k):
        j = lax.rem(z + k, NZ)
        return j, at(y, core, j, x)

    sibling = at(y, 1 - core, z, x)

    barrier = pltpu.get_barrier_semaphore()
    peers = [z_peer(k)[1] for k in NEAR_LAST[NZ]]
    peers += [frame_peer(k) for k in NEAR_LAST[8]]
    peers += [row_peer(1), row_peer(-1)]
    peers += [at(y, core, z, lax.rem(x + k, NX)) for k in range(1, NX)]
    for peer in peers:
        pl.semaphore_signal(barrier, inc=1, device_id=peer, device_id_type=MESH)

    loads = [
        pltpu.make_async_copy(s, d, wsem.at[i])
        for i, (s, d) in enumerate(
            [(lat, latn.at[0]), (cot, latn.at[1]), (wqkv_h, wqkv), (wout_h, wout), (wsp_h, wsp), (wt_h, wt), (seg_h, seg)]
        )
    ]
    for cp in loads:
        cp.start()

    def send(src, dst, ssem, rsem, peer):
        cp = pltpu.make_async_remote_copy(
            src_ref=src, dst_ref=dst, send_sem=ssem, recv_sem=rsem,
            device_id=peer, device_id_type=MESH,
        )
        cp.start()
        return cp

    latp[...] = jnp.zeros_like(latp)
    dp[...] = jnp.zeros_like(dp)

    def rows_of(i, dst):
        loads[i].wait()
        v = latn[i].astype(F32)
        for f in range(2):
            dst[f * WP : f * WP + W, :] = v[:, f, :]

    rows_of(0, latp)
    lv = latp[...]
    lv = lv * jax.nn.sigmoid(lv)
    act[1] = lv.astype(BF)
    hbuf[1] = pack2(lv).astype(BF)

    def to_pixels(src, dst):
        halves = [
            jnp.concatenate(
                [src[WP * f + 16 * j + 8 * h : WP * f + 16 * j + 8 * h + 8, :] for j in range(7) for f in range(2)]
                + [jnp.zeros((16, C), F32)],
                axis=0,
            )
            for h in range(2)
        ]
        dst[...] = pack2(jnp.concatenate(halves, axis=0)).astype(BF).reshape(8, 16, 2 * C)

    pl.semaphore_wait(barrier, len(peers))

    halo = [
        send(hbuf.at[1], hbuf.at[0], hs.at[0], hr.at[0], row_peer(1)),
        send(hbuf.at[1], hbuf.at[2], hs.at[1], hr.at[1], row_peer(-1)),
    ]

    def exchange(snd, rcv, ssem, rsem, base):
        cps = []
        for k in NEAR_LAST[8]:
            cps.append(
                send(snd.at[lax.rem(fr + k, 8)], rcv.at[fr],
                     ssem.at[base + k - 1], rsem.at[base + k - 1], frame_peer(k))
            )
        rcv[pl.ds(fr, 1)] = snd[pl.ds(fr, 1)]
        return cps

    rows_of(1, dp)
    to_pixels(dp, snd_c)
    cot_cps = exchange(snd_c, rcv_c, a_s, a_r, 0)

    loads[4].wait()
    for b in range(3):
        zbuf[b] = nn(act[1], wsp[1, b])
    for cp in halo:
        cp.wait_recv()

    def edges(ref):
        @pl.when(row == 0)
        def _():
            ref[0] = jnp.zeros((WP, 2 * C), BF)

        @pl.when(row == nrow - 1)
        def _():
            ref[2] = jnp.zeros((WP, 2 * C), BF)

    edges(hbuf)
    act[0] = unpack2(hbuf[0])
    act[2] = unpack2(hbuf[2])

    for b in range(3):
        zbuf[b] += nn(act[0], wsp[0, b]) + nn(act[2], wsp[2, b])
    rid = lax.broadcasted_iota(jnp.int32, (ROWS, C), 0)
    real = jnp.where(rid >= WP, rid - WP, rid) < W
    sp = latp[...] + pltpu.roll(zbuf[0], 1, 0) + zbuf[1] + pltpu.roll(zbuf[2], ROWS - 1, 0)
    zbuf[0] = jnp.where(real, sp, 0.0)
    to_pixels(zbuf.at[0], snd_s)
    sp_cps = exchange(snd_s, rcv_s, a_s, a_r, 7)

    for i in (2, 3, 5, 6):
        loads[i].wait()
    wo[...] = jnp.zeros_like(wo)
    wo[:C, :] = wout[...]
    for i in range(3):
        if i == 1:
            t = pltpu.roll(wqkv[:, 256:640].astype(F32), CP - 64, 1).astype(BF)
        else:
            t = wqkv[:, 640 * (i // 2) : 640 * (i // 2) + C]
        t = widen(t[:, :C])
        wq[i] = t
        if i > 0:
            wtr[i - 1] = t.T

    ri = lax.broadcasted_iota(jnp.int32, (UNIT, UNIT), 0)
    ci = lax.broadcasted_iota(jnp.int32, (UNIT, UNIT), 1)
    rseg = jnp.zeros((UNIT, UNIT), jnp.int32)
    cseg = jnp.zeros((UNIT, UNIT), jnp.int32)
    nxt = jnp.zeros((UNIT, UNIT), F32)
    prv = jnp.zeros((UNIT, UNIT), F32)
    for f in range(16):
        rseg = jnp.where(ri // 8 == f, seg[f], rseg)
        cseg = jnp.where(ci // 8 == f, seg[f], cseg)
        if f < 15:
            ok = jnp.where(seg[f] == seg[f + 1], 1.0, 0.0).astype(F32)
            nxt = jnp.where(ri // 8 == f, ok, nxt)
            prv = jnp.where(ri // 8 == f + 1, ok, prv)
    bias = jnp.where((rseg == cseg) & (ri % 8 == ci % 8), 0.0, -1e30)

    def wide(m):
        m = jnp.concatenate([m, m, m], axis=1)[:, :C]
        return jnp.concatenate([m, m], axis=0)

    nxt, prv = wide(nxt), wide(prv)
    scale = 1.0 / math.sqrt(C // HEADS)

    for cp in cot_cps:
        cp.wait_recv()
    for cp in sp_cps:
        cp.wait_recv()

    spf = unpack2(rcv_s[...].reshape(UNIT, 2 * C)).astype(F32)
    cotb = unpack2(rcv_c[...].reshape(UNIT, 2 * C))
    am = (spf * jax.nn.sigmoid(spf)).astype(BF)
    u_act[...] = am
    u_cot[...] = cotb
    tmp = spf + nn(am, wt[1])
    tmp = tmp + down8(nn(am, wt[0])) * prv
    tmp = tmp + up8(nn(am, wt[2])) * nxt
    tf = tmp.astype(BF).astype(F32)
    cen = tf - jnp.mean(tf, axis=-1, keepdims=True)
    inv = lax.rsqrt(jnp.mean(cen * cen, axis=-1, keepdims=True) + 1e-05)
    nhat = cen * inv
    nrm = nhat.astype(BF)
    u_nrm[...] = nrm
    qall = nn(nrm, wq[0]).astype(BF)
    kall = nn(nrm, wq[1]).astype(BF)
    vall = nn(nrm, wq[2]).astype(BF)
    kt = nt(wtr[0], nrm)
    vt = nt(wtr[1], nrm)
    dmall = nt(cotb, wo[...]).astype(BF)

    def attention(u):
        rows = slice(UNIT * u, UNIT * u + UNIT)
        state, mixt, dqt = [], [], []
        dk, dv = [None] * 3, [None] * 3
        for hd in range(HEADS):
            lo, hi = 40 * hd, 40 * hd + 40
            t0, t1 = lo // 128, -(-hi // 128)
            w0, w1 = 128 * t0, 128 * t1
            lane = lax.broadcasted_iota(jnp.int32, (UNIT, w1 - w0), 1) + w0
            sel = (lane >= lo) & (lane < hi)
            qm = jnp.where(sel, qall[rows, w0:w1].astype(F32), 0.0).astype(BF)
            dmm = jnp.where(sel, dmall[rows, w0:w1].astype(F32), 0.0).astype(BF)
            state.append((lo, hi, t0, t1, qm, dmm, nt(kall[rows, w0:w1], qm), nt(vall[rows, w0:w1], dmm)))
        second = []
        for lo, hi, t0, t1, qm, dmm, s, dpr in state:
            s = s * scale + bias
            e = jnp.exp(s - jnp.max(s, axis=0, keepdims=True))
            p = e * (1.0 / jnp.sum(e, axis=0, keepdims=True))
            ds = (p * (dpr - jnp.sum(p * dpr, axis=0, keepdims=True)) * scale).astype(BF)
            second.append((lo, hi, t0, t1, qm, dmm, p.astype(BF), ds))
        for lo, hi, t0, t1, qm, dmm, pb, ds in second:
            mixt.append(nn(vt[lo:hi, rows].astype(BF), pb))
            dqt.append(nn(kt[lo:hi, rows].astype(BF), ds))
            for acc, val in ((dk, nn(ds, qm)), (dv, nn(pb, dmm))):
                for t in range(t0, t1):
                    part = val[:, 128 * (t - t0) : 128 * (t - t0) + 128]
                    acc[t] = part if acc[t] is None else acc[t] + part
        u_mix[:, rows] = jnp.concatenate(mixt, axis=0).astype(BF)
        dq = widen(jnp.concatenate(dqt, axis=0).T)
        u_dq[rows, :] = pack3(dq, jnp.concatenate(dk, axis=1), jnp.concatenate(dv, axis=1)).astype(BF)

    attention(0)
    attention(1)
    dn = nt(u_dq[:, : 3 * C], wqkv[...])
    ln = inv * (
        dn
        - jnp.mean(dn, axis=-1, keepdims=True)
        - nhat * jnp.mean(dn * nhat, axis=-1, keepdims=True)
    )
    dt = (cotb.astype(F32) + ln).astype(BF)
    dtf = dt.astype(F32)
    carried = nt(dt, wt[1]) + up8(nt(dt, wt[0])) * nxt + down8(nt(dt, wt[2])) * prv
    snd_d[...] = pack2(dtf + silu_grad(spf) * carried).astype(BF).reshape(8, 16, 2 * C)
    d_cps = exchange(snd_d, rcv_d, a_s, a_r, 14)

    u_dt[...] = pack3(widen(up8(dtf) * nxt), widen(dtf), widen(down8(dtf) * prv)).astype(BF)
    g_t[0:C, :] = tn(u_act[...], u_dt[...]).astype(BF)
    g_t[C : 2 * C, :] = tn(u_nrm[...], u_dq[...]).astype(BF)
    go = widen(nn(u_mix[...], u_cot[...])).astype(BF)
    g_t[2 * C : 2 * C + 128, 768:] = jnp.zeros((128, 256), BF)
    for dst, lane, src, col, n in OUT_BLOCKS:
        g_t[dst : dst + n, lane : lane + 128] = go[src : src + n, col : col + 128]

    bufs = (g_t, g_s)
    outs = (f_t, f_s)
    half = [n // 2 for n in NR]
    quar = [MAIN // 2] * 2
    mine = [pl.multiple_of(core * n, 16) for n in half]
    other = [pl.multiple_of((1 - core) * n, 16) for n in half]
    low = [pl.multiple_of(i2 // 2 * n, 16) for n in quar]
    lane1 = pl.multiple_of(i1 * 256, 256)
    lane2 = pl.multiple_of(i2 % 2 * 128, 128)

    third = [n // 3 for n in half]

    def r0_start(b, c):
        rows = third[b]
        return [
            send(bufs[b].at[pl.ds(pl.multiple_of(other[b] + c * rows, 16), rows), pl.ds(512 * j, 512)],
                 r0.at[b, pl.ds(c * rows, rows), pl.ds(512 * j, 512)],
                 s0s.at[b, 2 * c + j], s0r.at[b, 2 * c + j], sibling)
            for j in range(2)
        ]

    def r0_finish(b, c, cps):
        for cp in cps:
            cp.wait_recv()
        rows = third[b]
        m = pl.ds(pl.multiple_of(mine[b] + c * rows, 16), rows)
        sl = slice(c * rows, c * rows + rows)
        p1[b, sl] = (bufs[b][m, :].astype(F32) + r0[b, sl].astype(F32)).astype(BF)

    def r1_start(b):
        cps = []
        for k in NEAR_LAST[4]:
            j, peer = first_peer(k)
            cps.append(
                send(p1.at[b, pl.ds(0, MAIN), pl.ds(pl.multiple_of(j * 256, 256), 256)],
                     r1.at[b, k - 1, pl.ds(0, MAIN)], s1s.at[b, k - 1], s1r.at[b, k - 1], peer)
            )
        return cps

    def r1_finish(b, cps):
        for cp in cps:
            cp.wait_recv()
        t = p1[b, : MAIN, pl.ds(lane1, 256)].astype(F32)
        for k in range(3):
            t = t + r1[b, k, : MAIN].astype(F32)
        p2[b, : MAIN] = t.astype(BF)

    def r2_start(b):
        cps = []
        for k in NEAR_LAST[4]:
            j, peer = second_peer(k)
            cps.append(
                send(p2.at[b, pl.ds(pl.multiple_of(j // 2 * quar[b], 16), quar[b]),
                           pl.ds(pl.multiple_of(j % 2 * 128, 128), 128)],
                     r2.at[b, k - 1, pl.ds(0, quar[b])], s2s.at[b, k - 1], s2r.at[b, k - 1], peer)
            )
        return cps

    def r2_finish(b, cps):
        for cp in cps:
            cp.wait_recv()
        t = p2[b, pl.ds(low[b], quar[b]), pl.ds(lane2, 128)].astype(F32)
        for k in range(3):
            t = t + r2[b, k, : quar[b]].astype(F32)
        p3[b, : quar[b]] = t.astype(BF)
        p3[b, quar[b] :] = jnp.zeros((256 - quar[b], 128), BF)

    def r3_start(b):
        cps = []
        for k in NEAR_LAST[NZ]:
            j, peer = z_peer(k)
            cps.append(
                send(p3.at[b, pl.ds(pl.multiple_of(j * 32, 32), 32)], r3.at[b, k - 1],
                     s3s.at[b, k - 1], s3r.at[b, k - 1], peer)
            )
        return cps

    zrow = pl.multiple_of(z * 32, 32)

    def r3_finish(b, cps):
        for cp in cps:
            cp.wait_recv()
        t = p3[b, pl.ds(zrow, 32)].astype(F32)
        for k in range(NZ - 1):
            t = t + r3[b, k].astype(F32)
        g3[b, pl.ds(zrow, 32)] = t.astype(BF)

    def g3_start(b):
        piece = g3.at[b, pl.ds(zrow, 32)]
        return [
            send(piece, piece, s3s.at[b + 2, k - 1], s3r.at[b + 2, k - 1], z_peer(k)[1])
            for k in NEAR_LAST[NZ]
        ]

    def g3_finish(b, cps):
        for cp in cps:
            cp.wait_recv()
        outs[b][pl.ds(pl.multiple_of(mine[b] + low[b], 16), quar[b]),
                pl.ds(pl.multiple_of(lane1 + lane2, 128), 128)] = g3[b, : quar[b]]

    def g2_start(b):
        piece = outs[b].at[pl.ds(pl.multiple_of(mine[b] + low[b], 16), quar[b]),
                           pl.ds(pl.multiple_of(lane1 + lane2, 128), 128)]
        return [
            send(piece, piece, s2s.at[b + 2, k - 1], s2r.at[b + 2, k - 1], second_peer(k)[1])
            for k in NEAR_LAST[4]
        ]

    def block(b, j):
        return outs[b].at[pl.ds(mine[b], MAIN), pl.ds(pl.multiple_of(j * 256, 256), 256)]

    def g1_start(b):
        piece = block(b, i1)
        return [
            send(piece, piece, s1s.at[b + 2, k - 1], s1r.at[b + 2, k - 1], first_peer(k)[1])
            for k in NEAR_LAST[4]
        ]

    def g0_start(b, k):
        lanes = pl.ds(pl.multiple_of(lax.rem(i1 - k + 4, 4) * 256, 256), 256)
        cps = []
        for c in range(3):
            rows = pl.ds(pl.multiple_of(mine[b] + c * (MAIN // 3), 16), MAIN // 3)
            piece = outs[b].at[rows, lanes]
            cps.append(send(piece, piece, s0s.at[b + 2, 3 * k + c], s0r.at[b + 2, 3 * k + c], sibling))
        return cps

    def got(cps):
        for cp in cps:
            cp.wait_recv()

    zlane = pl.multiple_of(z * 128, 128)
    rest = pl.ds(pl.multiple_of(mine[1] + MAIN, 16), REST)

    def z1_start():
        cps = []
        for k in NEAR_LAST[NZ]:
            j, peer = z_peer(k)
            cps.append(
                send(p1.at[1, pl.ds(MAIN, REST), pl.ds(pl.multiple_of(j * 128, 128), 128)],
                     zr.at[k - 1], zs.at[0, k - 1], zv.at[0, k - 1], peer)
            )
        return cps

    def z1_finish(cps):
        got(cps)
        t = p1[1, MAIN : MAIN + REST, pl.ds(zlane, 128)].astype(F32)
        for k in range(NZ - 1):
            t = t + zr[k].astype(F32)
        zx[pl.ds(i1, 1)] = t.astype(BF)[None]

    def spread(ref, place, sem, peer_of):
        piece = ref.at[place]
        return [
            send(piece, piece, zs.at[sem, k - 1], zv.at[sem, k - 1], peer_of(k)[1])
            for k in NEAR_LAST[4]
        ]

    def in_order(ref):
        t = ref[0].astype(F32)
        for k in range(1, 4):
            t = t + ref[k].astype(F32)
        return t.astype(BF)

    def z4_start():
        piece = f_s.at[rest, pl.ds(zlane, 128)]
        return [
            send(piece, piece, zs.at[3, k - 1], zv.at[3, k - 1], z_peer(k)[1])
            for k in NEAR_LAST[NZ]
        ]

    def z0_start():
        cps = []
        for j in range(2):
            piece = f_s.at[rest, pl.ds(512 * j, 512)]
            cps.append(send(piece, piece, s0s.at[3, 12 + j], s0r.at[3, 12 + j], sibling))
        return cps

    sent = []

    def keep(cps):
        sent.extend(cps)
        return cps

    t0c = [keep(r0_start(0, c)) for c in range(3)]
    for c in range(3):
        r0_finish(0, c, t0c[c])
    t1c = keep(r1_start(0))

    got(d_cps)
    t = unpack2(rcv_d[...].reshape(UNIT, 2 * C)).astype(F32)
    dv = jnp.concatenate(
        [
            t[UNIT * h + 16 * j + 8 * f : UNIT * h + 16 * j + 8 * f + 8]
            for f in range(2) for j in range(7) for h in range(2)
        ],
        axis=0,
    )
    dp[...] = dv
    dbuf[1] = dv.astype(BF)
    dhb[1] = pack2(dv).astype(BF)
    dcat = pack3(
        widen(pltpu.roll(dv, ROWS - 1, 0)), widen(dv), widen(pltpu.roll(dv, 1, 0))
    ).astype(BF)
    s0c = []
    for a in range(3):
        t = tn(act[a], dcat).astype(BF)
        for c in range(2):
            g_s[c * half[1] + a * 160 : c * half[1] + a * 160 + 160, :] = t[160 * c : 160 * c + 160]
        s0c.append(keep(r0_start(1, a)))
    for a in range(3):
        r0_finish(1, a, s0c[a])
    s1c = keep(r1_start(1))
    z1c = keep(z1_start())
    r1_finish(0, t1c)
    t2c = keep(r2_start(0))
    r2_finish(0, t2c)
    t3c = keep(r3_start(0))
    r1_finish(1, s1c)
    s2c = keep(r2_start(1))
    dhalo = [
        send(dhb.at[1], dhb.at[0], dhs.at[0], dhr.at[0], row_peer(1)),
        send(dhb.at[1], dhb.at[2], dhs.at[1], dhr.at[1], row_peer(-1)),
    ]
    z1_finish(z1c)
    z2c = keep(spread(zx, i1, 1, first_peer))
    r3_finish(0, t3c)
    t4c = keep(g3_start(0))
    r2_finish(1, s2c)
    s3c = keep(r3_start(1))
    got(z2c)
    zy[pl.ds(i2, 1)] = in_order(zx)[None]
    z3c = keep(spread(zy, i2, 2, second_peer))
    g3_finish(0, t4c)
    t5c = keep(g2_start(0))

    got(dhalo)

    edges(dhb)
    dbuf[0] = unpack2(dhb[0])
    dbuf[2] = unpack2(dhb[2])

    for b in range(3):
        zbuf[b] = nt(dbuf[2], wsp[0, b]) + nt(dbuf[1], wsp[1, b]) + nt(dbuf[0], wsp[2, b])
    da = pltpu.roll(zbuf[0], ROWS - 1, 0) + zbuf[1] + pltpu.roll(zbuf[2], 1, 0)
    t = dp[...] + silu_grad(latp[...]) * da
    gi[...] = jnp.stack([t[:W], t[WP : WP + W]], axis=1).astype(BF)

    r3_finish(1, s3c)
    s4c = keep(g3_start(1))
    got(z3c)
    f_s[rest, pl.ds(zlane, 128)] = in_order(zy)
    got(t5c)
    t6c = keep(g1_start(0))
    t7c = g0_start(0, 0)
    g3_finish(1, s4c)
    s5c = keep(g2_start(1))
    z4c = keep(z4_start())
    got(s5c)
    s6c = keep(g1_start(1))
    s7c = g0_start(1, 0)
    for cp, k in zip(t6c, NEAR_LAST[4]):
        cp.wait_recv()
        t7c += g0_start(0, k)
    got(z4c)
    s7c += z0_start()
    for cp, k in zip(s6c, NEAR_LAST[4]):
        cp.wait_recv()
        s7c += g0_start(1, k)
    got(t7c)
    for b, t in enumerate(unpack(f_t[0:C, :].astype(F32) * factor)):
        out_t[b] = t
    out_q[...] = (f_t[C : 2 * C, :].astype(F32) * factor)[:, : 3 * C]
    for dst, lane, src, col, n in OUT_BLOCKS:
        w = min(128, C - col)
        out_o[src : src + n, col : col + w] = f_t[dst : dst + n, lane : lane + w].astype(F32) * factor
    keep(t7c + s7c)
    got(s7c)
    for cp in halo + cot_cps + sp_cps + d_cps + dhalo + sent:
        cp.wait_send()


def finish(factor, gi, vt, vq, vo, fs, gin, gs, gt, gq, go, vs, sem):
    cps = []

    def out(src, dst):
        cp = pltpu.make_async_copy(src, dst, sem.at[len(cps)])
        cp.start()
        cps.append(cp)

    for b in range(3):
        out(vt.at[b], gt.at[b])
    for i in range(4):
        r = slice(80 * i, 80 * i + 80)
        out(vq.at[r], gq.at[r])
    out(vo, go)
    out(gi, gin)
    for a in range(3):
        for c in range(2):
            r = c * (NR[1] // 2) + 160 * a
            for b, t in enumerate(unpack(fs[r : r + 160, :].astype(F32) * factor)):
                vs[a, b, 160 * c : 160 * c + 160, :] = t
        for b in range(3):
            out(vs.at[a, b], gs.at[a, b])
    for cp in cps:
        cp.wait()


def on_device(latents, segments, w_spatial, w_temporal, w_qkv, w_out, cotangent):
    vm = pl.BlockSpec(memory_space=pltpu.VMEM)
    anyspec = pl.BlockSpec(memory_space=pl.ANY)
    dma = pltpu.SemaphoreType.DMA
    V = pltpu.VMEM
    hm = max(NR) // 2

    def by_column(t):
        return jnp.transpose(t.reshape(2, W, C), (1, 0, 2))

    factor = 1.0 / math.sqrt(54272)
    shapes = [(3, 3, C, C), (3, C, C), (C, 3 * C), (C, C)]
    inner = pl.pallas_call(
        lambda *refs: mega(factor, *refs),
        out_shape=(jax.ShapeDtypeStruct((W, 2, C), BF),)
        + tuple(jax.ShapeDtypeStruct(s, F32) for s in shapes[1:])
        + (jax.ShapeDtypeStruct((NR[1], GL), BF),),
        in_specs=[pl.BlockSpec(memory_space=pltpu.HBM)] * 7,
        out_specs=(vm,) * 5,
        scratch_shapes=[
            pltpu.SMEM((16,), jnp.int32), V((3, 3, C, C), BF), V((3, C, C), BF), V((C, 3 * C), BF), V((3, C, CP), BF),
            V((2, CP, C), BF), V((C, C), BF), V((CP, C), BF),
            V((2, W, 2, C), BF), V((ROWS, C), F32), V((3, ROWS, C), BF),
            V((3, WP, 2 * C), BF), V((3, WP, 2 * C), BF), V((3, ROWS, C), F32),
            V((8, 16, 2 * C), BF), V((8, 16, 2 * C), BF), V((8, 16, 2 * C), BF), V((8, 16, 2 * C), BF),
            V((2 * UNIT, C), BF), V((2 * UNIT, GL), BF), V((2 * UNIT, C), BF), V((2 * UNIT, GL), BF),
            V((C, 2 * UNIT), BF), V((2 * UNIT, C), BF),
            V((8, 16, 2 * C), BF), V((8, 16, 2 * C), BF),
            V((ROWS, C), F32), V((3, ROWS, C), BF),
            V((NR[0], GL), BF), V((NR[1], GL), BF),
            V((2, hm, GL), BF), V((2, 3, MAIN, 256), BF), V((2, 3, MAIN // 2, 128), BF),
            V((2, NZ - 1, 32, 128), BF),
            V((2, hm, GL), BF), V((2, MAIN, 256), BF), V((2, 256, 128), BF), V((2, 256, 128), BF),
            V((NR[0], GL), BF), V((NZ - 1, REST, 128), BF), V((4, REST, 128), BF), V((4, REST, 128), BF),
            dma((7,)), dma((2,)), dma((2,)), dma((21,)), dma((21,)), dma((2,)), dma((2,)),
            dma((4, 14)), dma((4, 14)), dma((4, 3)), dma((4, 3)), dma((4, 3)), dma((4, 3)),
            dma((4, NZ - 1)), dma((4, NZ - 1)), dma((4, NZ - 1)), dma((4, NZ - 1)),
        ],
        compiler_params=pltpu.CompilerParams(
            collective_id=0, has_side_effects=True, vmem_limit_bytes=40 * 1024 * 1024
        ),
        name="mega",
    )(*(
        pltpu.with_memory_space_constraint(t, pltpu.HBM)
        for t in (segments, by_column(latents), by_column(cotangent), w_spatial, w_temporal, w_qkv, w_out)
    ))
    gin, gs, gt, gq, go = pl.pallas_call(
        lambda *refs: finish(factor, *refs),
        out_shape=(jax.ShapeDtypeStruct((W, 2, C), BF),)
        + tuple(jax.ShapeDtypeStruct(s, F32) for s in shapes),
        in_specs=[vm] * 5,
        out_specs=(anyspec,) * 5,
        scratch_shapes=[V(shapes[0], F32), dma((18,))],
        compiler_params=pltpu.CompilerParams(vmem_limit_bytes=40 * 1024 * 1024),
        name="finish",
    )(*inner)
    gin = jnp.transpose(gin, (1, 0, 2)).reshape(latents.shape)
    return gin, gs, gt, gq, go


def solution(mesh):
    in_specs = (
        P("frame", "row", None, None),
        P(),
        P(),
        P(),
        P(),
        P(),
        P("frame", "row", None, None),
    )
    out_specs = (P("frame", "row", None, None), P(), P(), P(), P())
    return jax.shard_map(
        on_device, mesh=mesh, in_specs=in_specs, out_specs=out_specs, check_vma=False
    )
```
